32 devices in a mesh: groups: 2 (over y), row: 4 (over z), col: 2 (over x), depth: 2 (over core).
Axes of the slice: x: 2, y: 2, z: 4, core: 2. Of those that a mesh axis runs over, the one named last changes fastest.
Arguments:
- blocks: bfloat16 [64, 20, 64, 64], P(('groups', 'row', 'col')), parts along dimension 0, may hold values from -6 to 6
- pattern: int32 [64, 20], P(('groups', 'row', 'col')), parts along dimension 0, may hold values from 0 to 31, as said below
- owner_map: int32 [2, 64, 10, 1], P('depth', ('groups', 'row', 'col')), parts along dimension 1, may hold values from 0 to 7; in each aligned block of 40 rows (0 to 39, 40 to 79, ..., all dimensions but the last counted through in order) at most 16 rows name the same one
Outputs:
- regrouped: bfloat16 [2, 16, 8, 16, 64, 64], P('depth', ('groups', 'row', 'col')), parts along dimension 1
The draws below stay inside these ranges and needn't reach their ends.
There are 2 independent parts, one for each index of `groups`. The reference program is written for one: setup_inputs(seed, part) draws one part's arguments, and reference() takes and returns one part's arrays. A program takes and returns all parts, laid end to end along the dimension named above; each array names one. Nothing has to cross between parts.
Inputs may be any that keep to these rules, and one draw needn't show every extreme that they name: `pattern`: the 20 block columns of a block row are distinct and lie within 12 block positions of the row's own index, counted around the ends. `owner_map`: within one half and one aligned block of 4 block rows, no owner is named more than 16 times.
All inputs are finite; a program needn't handle non-finite values.
Results may differ from the reference program's by a relative error of at most 0.0049.
Values may be sent and summed in bfloat16 or wider, within the bound.
A program may use at most 64 MiB of HBM per device.

```python
import math
import jax
import jax.numpy as jnp
import numpy as np
from jax import lax

B = 64
K = 20
KH = 10
BR_DEV = 4
HOPS = 3
NB = 32
CAP = 16
N_ROW = 4
N_COL = 2


def draw_pattern(key, part):
    key = jax.random.fold_in(key, 7)
    reach = HOPS * BR_DEV
    window = 2 * reach + 1
    scores = jax.random.randint(key, (NB, window), 0, 1 << 20)
    scores = scores * window + jnp.arange(window, dtype=jnp.int32)[None, :]
    chosen = jnp.argsort(scores, axis=1, stable=True)[:, :K].astype(jnp.int32)
    return ((jnp.arange(NB, dtype=jnp.int32)[:, None] + chosen - reach) % NB).astype(jnp.int32)


def level_of(key, shape, cuts, low, high):
    level = 1.0
    for position, parts in cuts:
        heights = jax.random.uniform(jax.random.fold_in(jax.random.fold_in(key, 6), position), (parts,), jnp.float32, low / len(cuts), high / len(cuts))
        level = level * jnp.repeat(jnp.exp(heights), shape[position] // parts).reshape((-1,) + (1,) * (len(shape) - 1 - position))
    return level


def routed_block(key, own, number, rows, number_of, top, limit, lean):
    sequence = jax.random.permutation(key, number_of)
    crowded, usual = load_shares(number_of, rows * top, limit, lean, True), load_shares(number_of, rows * top, limit, lean, False)
    places = jnp.arange(number_of)

    def named(sizes, rotation):
        used = int((sizes > 0).sum())
        fixed = max(1, used // 4)
        moved = fixed + (places - fixed + rotation * (used - fixed)) % max(1, number_of - fixed)
        return jnp.zeros((number_of,), jnp.int32).at[sequence[jnp.where(places < fixed, places, moved)]].set(jnp.asarray(sizes, jnp.int32))

    sizes = jnp.where(number % 4 == 0, named(crowded, number // 4), named(usual, number - number // 4 - 1))
    mixed = jax.random.permutation(jax.random.fold_in(own, 3), number_of)
    donor, taker = mixed[0:number_of // 2 * 2:2], mixed[1:number_of // 2 * 2:2]
    margin = jnp.minimum(sizes[donor] - 1, limit - sizes[taker]) // 2
    margin = jnp.where((donor == sequence[0]) | (taker == sequence[0]) | (sizes[taker] == 0), 0, jnp.maximum(margin, 0))
    moved = jax.random.randint(jax.random.fold_in(own, 4), (number_of // 2,), 0, 1 << 20) % (margin + 1)
    sizes = sizes.at[donor].add(-moved).at[taker].add(moved)
    labels = jnp.searchsorted(jnp.cumsum(sizes), jnp.arange(rows * top), side="right").astype(jnp.int32)
    grid = labels.reshape(top, rows).T
    grid = grid[jax.random.permutation(jax.random.fold_in(own, 1), rows)]
    rotation = jax.random.randint(jax.random.fold_in(own, 2), (rows, 1), 0, top)
    return jnp.take_along_axis(grid, (jnp.arange(top)[None, :] + rotation) % top, axis=1)


def load_shares(number_of, total, bound, skew, full):
    weights = [(1 << 20) // math.isqrt(rank ** skew) + 1 for rank in range(1, number_of + 1)]
    largest = bound if full else min(bound, max(-(-total // number_of), total * weights[0] // sum(weights)))
    least = 1 if total - largest >= number_of - 1 else 0
    holding, spare = [largest] + [least] * (number_of - 1), total - largest - least * (number_of - 1)
    while spare > 0:
        movable = [i for i in range(1, number_of) if holding[i] < largest] or [i for i in range(1, number_of) if holding[i] < bound]
        mass, remaining = sum([weights[i] for i in movable]), spare
        for i in movable:
            extra = min(bound - holding[i], max(1, remaining * weights[i] // mass), spare)
            holding[i] = holding[i] + extra
            spare = spare - extra
    return np.array(holding)


def bell_draw(stream_key, dims, spread, limit, pieces=(), kind=jnp.bfloat16):
    entries = jax.random.normal(stream_key, dims, jnp.float32) * spread
    if len(pieces) > 0:
        entries = level_of(stream_key, dims, pieces, -0.22, 0.18) * entries
    return jnp.clip(entries, min=-limit, max=limit).astype(kind)


def setup_inputs(seed: int = 0, part: int = 0) -> dict:
    arg_keys = jax.random.split(jax.random.key(seed), 4)
    own_keys = jax.random.split(jax.random.fold_in(arg_keys[3], part), 4)
    blocks = bell_draw(own_keys[0], (NB, K, B, B), 1.0, 6.0, ((0, 8),))
    pattern = draw_pattern(jax.random.fold_in(jax.random.fold_in(arg_keys[3], part), 71), part)
    owner_map_keys = jax.random.split(jax.random.fold_in(own_keys[2], 1), 2 * NB * KH // (BR_DEV * KH))
    owner_map_turns = jax.random.permutation(jax.random.fold_in(own_keys[2], 3), 2 * NB * KH // (BR_DEV * KH))
    owner_map = jax.vmap(lambda own, number: routed_block(jax.random.fold_in(own_keys[2], 2), own, number, BR_DEV * KH, N_ROW * N_COL, 1, CAP, 2))(owner_map_keys, owner_map_turns).reshape((2, NB, KH, 1))
    return {"blocks": blocks, "pattern": pattern, "owner_map": owner_map}


def filtered_product(left, right, pattern):
    slot_count = pattern.shape[1]
    block_size = left.shape[2]

    def one_row(row_index):
        own_pattern = pattern[row_index]
        fetched = right[own_pattern].astype(jnp.float32).reshape(slot_count, slot_count, block_size * block_size)
        fetched_pattern = pattern[own_pattern]
        select = (fetched_pattern[:, None, :] == own_pattern[None, :, None]).astype(jnp.float32)
        aligned = jnp.einsum('kjl,klx->kjx', select, fetched, precision=lax.Precision.HIGHEST)
        aligned = aligned.reshape(slot_count, slot_count, block_size, block_size)
        return jnp.einsum('kab,kjbc->jac', left[row_index].astype(jnp.float32), aligned, precision=lax.Precision.HIGHEST)
    return lax.map(one_row, jnp.arange(pattern.shape[0], dtype=jnp.int32))

def reference(blocks, pattern, owner_map):
    inv_scale = 1.0 / math.sqrt(B * K)
    squared = (filtered_product(blocks, blocks, pattern) * inv_scale).astype(jnp.bfloat16)
    cubic_term = filtered_product(blocks, squared, pattern)
    updated = (1.5 * blocks.astype(jnp.float32) - 0.5 * inv_scale * cubic_term).astype(jnp.bfloat16)
    owner_count = N_ROW * N_COL
    item_count = BR_DEV * KH
    halves = []
    for half_index in range(2):
        item_blocks = updated[:, half_index * KH:(half_index + 1) * KH].reshape(owner_count, item_count, B * B)
        targets = owner_map[half_index, :, :, 0].reshape(owner_count, item_count)

        def place(row_data):
            source_items, source_targets = row_data
            same_owner = source_targets[:, None] == source_targets[None, :]
            rank_index = lax.optimization_barrier(jnp.sum(jnp.tril(same_owner, -1).astype(jnp.int32), axis=1))
            destination = (source_targets * CAP + rank_index).astype(jnp.int32)
            return jnp.zeros((owner_count * CAP, B * B), jnp.bfloat16).at[destination].set(source_items)
        buckets = lax.map(place, (item_blocks, targets))
        buckets = buckets.reshape(owner_count, owner_count, CAP, B, B).transpose(1, 0, 2, 3, 4)
        halves.append(buckets)
    return jnp.stack(halves)
```

```python
import functools
import math

import jax
import jax.numpy as jnp
from jax import lax
from jax.experimental import pallas as pl
from jax.experimental.pallas import tpu as pltpu
from jax.sharding import PartitionSpec as P

HOPS = 3
MESH = pl.DeviceIdType.MESH


def passed_along(value, axis, by):
    peers = lax.axis_size(axis)
    return lax.ppermute(value, axis, [(i, (i + by) % peers) for i in range(peers)])


def product_rows(left, left_pattern, local_index, near_blocks, near_pattern, first_slot, slot_span):
    slot_count = left.shape[1]
    block_size = left.shape[2]

    def one_row(row_data):
        own_blocks, own_pattern, own_local = row_data
        used_local = lax.dynamic_slice_in_dim(own_local, first_slot, slot_span, 0)
        used_blocks = lax.dynamic_slice_in_dim(own_blocks, first_slot, slot_span, 0)
        fetched = jnp.take(near_blocks, used_local, axis=0).reshape(
            slot_span, slot_count, block_size * block_size
        )
        fetched_pattern = jnp.take(near_pattern, used_local, axis=0)
        select = (fetched_pattern[:, None, :] == own_pattern[None, :, None]).astype(jnp.bfloat16)
        aligned = jnp.einsum("kjl,klx->kjx", select, fetched, preferred_element_type=jnp.bfloat16)
        aligned = aligned.reshape(slot_span, slot_count, block_size, block_size)
        return jnp.einsum("kab,kjbc->jac", used_blocks, aligned, preferred_element_type=jnp.float32)

    return lax.map(one_row, (left, left_pattern, local_index))


def regroup(updated, targets):
    device_count = lax.axis_size(("row", "col"))
    row_count = updated.shape[0]
    half_slots = updated.shape[1]
    block_size = updated.shape[2]
    item_count = row_count * half_slots
    capacity = max(2, 3 * item_count // device_count + 1)
    flat_targets = targets.reshape(item_count)
    same_owner = flat_targets[:, None] == flat_targets[None, :]
    earlier = jnp.arange(item_count)[:, None] > jnp.arange(item_count)[None, :]
    rank_index = jnp.sum((same_owner & earlier).astype(jnp.int32), axis=1)
    destination = flat_targets * capacity + rank_index
    select = (
        jnp.arange(device_count * capacity, dtype=jnp.int32)[:, None] == destination[None, :]
    ).astype(jnp.bfloat16)
    outgoing = jnp.dot(
        select,
        updated.reshape(item_count, block_size * block_size),
        preferred_element_type=jnp.float32,
    ).astype(jnp.bfloat16)
    outgoing = outgoing.reshape(device_count, capacity, block_size, block_size)
    received = lax.all_to_all(outgoing, ("row", "col"), split_axis=0, concat_axis=0, tiled=True)
    return received.reshape(1, 1, device_count, capacity, block_size, block_size)


def shards(blocks, pattern, owner_map):
    row_count = blocks.shape[0]
    slot_count = blocks.shape[1]
    block_size = blocks.shape[2]
    half_slots = slot_count // 2
    device_count = lax.axis_size(("row", "col"))
    total_rows = device_count * row_count
    position = lax.axis_index(("row", "col"))
    layer_index = lax.axis_index("depth")
    inv_scale = 1.0 / math.sqrt(block_size * slot_count)
    targets = owner_map[0, :, :, 0]
    offsets = list(range(HOPS, 0, -1)) + list(range(-1, -HOPS - 1, -1))
    arrivals = [passed_along((blocks, pattern), ("row", "col"), offset) for offset in offsets]
    near_blocks = jnp.concatenate(
        [arrived[0] for arrived in arrivals[:HOPS]]
        + [blocks]
        + [arrived[0] for arrived in arrivals[HOPS:]],
        axis=0,
    )
    near_pattern = jnp.concatenate(
        [arrived[1] for arrived in arrivals[:HOPS]]
        + [pattern]
        + [arrived[1] for arrived in arrivals[HOPS:]],
        axis=0,
    )
    first_row = (position - HOPS) * row_count
    local_index = (pattern - first_row) % total_rows
    first_slot = layer_index * half_slots
    partial_value = product_rows(
        blocks, pattern, local_index, near_blocks, near_pattern, first_slot, half_slots
    )
    squared = (lax.psum(partial_value, "depth") * inv_scale).astype(jnp.bfloat16)
    w_arrivals = [passed_along(squared, ("row", "col"), offset) for offset in offsets]
    near_squared = jnp.concatenate(w_arrivals[:HOPS] + [squared] + w_arrivals[HOPS:], axis=0)
    partial_value = product_rows(
        blocks, pattern, local_index, near_squared, near_pattern, first_slot, half_slots
    )
    cubic_term = lax.psum_scatter(
        partial_value.astype(jnp.bfloat16), "depth", scatter_dimension=1, tiled=True
    ).astype(jnp.float32)
    own_blocks = lax.dynamic_slice_in_dim(blocks, first_slot, half_slots, 1)
    updated = (1.5 * own_blocks.astype(jnp.float32) - 0.5 * inv_scale * cubic_term).astype(
        jnp.bfloat16
    )
    return regroup(updated, targets)


def gather_kernel(
    dims, blocks_ref, meta_ref, packed, meta_v,
    send_sem, recv_sem, sib_sem, meta_send, meta_recv,
):
    n_row, n_col, rows, slots, size, capacity = dims
    devices = n_row * n_col
    part = rows * size
    half_rows = slots // 2 * size
    z, x, h = lax.axis_index("row"), lax.axis_index("col"), lax.axis_index("depth")
    me = z * n_col + x
    across = n_col - 1 - x

    def device(to_z, to_x, to_h):
        return {"row": to_z, "col": to_x, "depth": to_h}

    sibling = device(z, x, 1 - h)

    barrier = pltpu.get_barrier_semaphore()
    for step in range(1, devices):
        peer = lax.rem(me + step, devices)
        pl.semaphore_signal(
            barrier, inc=1, device_id=device(peer // n_col, lax.rem(peer, n_col), h),
            device_id_type=MESH,
        )
    pl.semaphore_signal(barrier, inc=1, device_id=sibling, device_id_type=MESH)

    for pair in range(rows // 2):
        packed[me, : slots * size, pair * 2 * size : (pair + 1) * 2 * size] = jnp.concatenate(
            [blocks_ref[2 * pair + t].reshape(slots * size, size) for t in range(2)], axis=1
        )
    for source in range(devices):
        packed[source, slots * size :, :] = jnp.zeros((size, part), jnp.bfloat16)
    meta_v[me] = meta_ref[...]
    pl.semaphore_wait(barrier, devices)

    def meta_copy(step):
        peer = lax.rem(me + step, devices)
        return pltpu.make_async_remote_copy(
            src_ref=meta_v.at[me], dst_ref=meta_v.at[me],
            send_sem=meta_send.at[step], recv_sem=meta_recv.at[step],
            device_id=device(peer // n_col, lax.rem(peer, n_col), h), device_id_type=MESH,
        )

    def piece(position, which):
        return packed.at[position, pl.ds(which * half_rows, half_rows), :]

    def copy(position, k, target, landed, which=None):
        ref = piece(position, h if which is None else which)
        return pltpu.make_async_remote_copy(
            src_ref=ref, dst_ref=ref, send_sem=send_sem.at[position, k],
            recv_sem=landed.at[position], device_id=target, device_id_type=MESH,
        )

    sends = []

    def start(valid, position, k, target, landed):
        @pl.when(valid)
        def _():
            copy(position, k, target, landed).start()
        sends.append((valid, position, k, target, landed))

    for step in range(1, devices):
        meta_copy(step).start()
    start(z > 0, me, 0, device(z - 1, x, h), recv_sem)
    start(z < n_row - 1, me, 1, device(z + 1, x, h), recv_sem)
    start(z >= 0, me, 2, device(z, across, h), recv_sem)

    def from_z(distance, way):
        source = z + way * distance
        valid = (source >= 0) & (source < n_row)
        position = source * n_col + x

        @pl.when(valid)
        def _():
            copy(position, 0, sibling, recv_sem).wait_recv()
        start(valid & (z - way >= 0) & (z - way < n_row), position, 0, device(z - way, x, h), recv_sem)
        start(valid, position, 1, device(z, across, h), recv_sem)
        start(valid, position, 2, sibling, sib_sem)

    def from_x(distance, way):
        source = z + way * distance
        valid = (source >= 0) & (source < n_row)
        position = source * n_col + across

        @pl.when(valid)
        def _():
            copy(position, 0, sibling, recv_sem).wait_recv()
        start(valid, position, 0, sibling, sib_sem)

    for distance in range(1, n_row):
        from_z(distance, 1)
        from_z(distance, -1)
        if distance == 1:
            from_x(0, 1)
        else:
            from_x(distance - 1, 1)
            from_x(distance - 1, -1)
    from_x(n_row - 1, 1)
    from_x(n_row - 1, -1)

    for step in range(1, devices):
        meta_copy(step).wait()
    for step in range(1, devices):
        position = lax.rem(me + step, devices)
        copy(position, 0, sibling, sib_sem, 1 - h).wait_recv()
    for valid, position, k, target, landed in sends:
        @pl.when(valid)
        def _(position=position, k=k, target=target, landed=landed):
            copy(position, k, target, landed).wait_send()


def dense_kernel(dims, packed, meta_s, out_ref, x_ref, sq_ref, mask_ref, up_ref):
    n_row, n_col, rows, slots, size, capacity = dims
    devices = n_row * n_col
    total = devices * rows
    width = total * size
    part = rows * size
    me = lax.axis_index("row") * n_col + lax.axis_index("col")

    lane = lax.broadcasted_iota(jnp.int32, (1, 2 * size), 1)

    def expand(source, carry):
        for row in range(rows):
            lanes = row // 2 * 2 * size
            at = row % 2 * size
            for pair in range(total // 2):
                slot = [meta_s[source, 0, row * total + 2 * pair + t] for t in range(2)]
                both = [
                    packed[source, pl.ds(pl.multiple_of(slot[t] * size, size), size), lanes : lanes + 2 * size]
                    for t in range(2)
                ]
                spot = slice(pair * 2 * size, (pair + 1) * 2 * size)
                x_ref[pl.ds(pl.multiple_of(source * part + row * size, size), size), spot] = (
                    jnp.concatenate([both[t][:, at : at + size] for t in range(2)], axis=1)
                )
                kept = [(slot[t] < slots).astype(jnp.float32) for t in range(2)]
                mask_ref[source, row : row + 1, spot] = jnp.where(lane < size, kept[0], kept[1])
        return carry

    lax.fori_loop(0, devices, expand, 0)

    inv_scale = 1.0 / math.sqrt(size * slots)
    tile = 4 * 2 * size

    def square(source, carry):
        own = pl.ds(pl.multiple_of(source * part, part), part)
        for column in range(width // tile):
            spot = slice(column * tile, (column + 1) * tile)
            value = jnp.dot(x_ref[own, :], x_ref[:, spot], preferred_element_type=jnp.float32)
            kept = jnp.broadcast_to(mask_ref[source, :, spot][:, None, :], (rows, size, tile))
            sq_ref[own, spot] = (value * inv_scale * kept.reshape(part, tile)).astype(jnp.bfloat16)
        return carry

    lax.fori_loop(0, devices, square, 0)

    def cube(source, carry):
        own = pl.ds(pl.multiple_of(source * part, part), part)
        for column in range(width // tile):
            spot = slice(column * tile, (column + 1) * tile)
            value = jnp.dot(x_ref[own, :], sq_ref[:, spot], preferred_element_type=jnp.float32)
            value = 1.5 * x_ref[own, spot].astype(jnp.float32) - (0.5 * inv_scale) * value
            value = value.astype(jnp.bfloat16)
            for t in range(4):
                up_ref[column * 4 + t] = value[:, t * 2 * size : (t + 1) * 2 * size]
        for rank in range(capacity):
            code = meta_s[source, 1, me * capacity + rank]
            found = jnp.maximum(code, 0)
            column = found & (total - 1)
            row = found >> (total.bit_length() - 1)
            block = up_ref[column >> 1, pl.ds(pl.multiple_of(row * size, size), size), :]
            block = block.astype(jnp.float32)
            block = jnp.where((column & 1) == 0, block[:, :size], block[:, size:])
            out_ref[source, rank] = jnp.where(code >= 0, block, 0.0).astype(jnp.bfloat16)
        return carry

    lax.fori_loop(0, devices, cube, 0)


def dense_shards(blocks, pattern, owner_map):
    rows, slots, size, _ = blocks.shape
    n_row, n_col = lax.axis_size("row"), lax.axis_size("col")
    devices = n_row * n_col
    total = devices * rows
    items = rows * (slots // 2)
    capacity = max(2, 3 * items // devices + 1)
    h = lax.axis_index("depth")

    slot_number = jnp.arange(slots, dtype=jnp.int32)[None, :, None]
    named = pattern[:, :, None] == jnp.arange(total, dtype=jnp.int32)[None, None, :]
    slot_of = slots + jnp.sum(jnp.where(named, slot_number - slots, 0), axis=1)

    targets = owner_map.reshape(items)
    earlier = jnp.arange(items)[:, None] > jnp.arange(items)[None, :]
    rank = jnp.sum(((targets[:, None] == targets[None, :]) & earlier).astype(jnp.int32), axis=1)
    columns = lax.dynamic_slice_in_dim(pattern, h * (slots // 2), slots // 2, 1)
    code = jnp.arange(rows, dtype=jnp.int32)[:, None] * total + columns
    placed = jnp.arange(devices * capacity, dtype=jnp.int32)[:, None] == (targets * capacity + rank)[None, :]
    item_at = jnp.sum(jnp.where(placed, code.reshape(1, items) + 1, 0), axis=1) - 1
    lanes = 128
    meta = jnp.concatenate(
        [slot_of.reshape(1, lanes), item_at.reshape(1, lanes), jnp.zeros((6, lanes), jnp.int32)], axis=0
    )
    dims = (n_row, n_col, rows, slots, size, capacity)
    width = total * size
    vmem = pl.BlockSpec(memory_space=pltpu.VMEM)
    gathered, gathered_meta = pl.pallas_call(
        functools.partial(gather_kernel, dims),
        out_shape=(
            jax.ShapeDtypeStruct((devices, (slots + 1) * size, rows * size), jnp.bfloat16),
            jax.ShapeDtypeStruct((devices, 8, lanes), jnp.int32),
        ),
        in_specs=[vmem, vmem],
        out_specs=(vmem, vmem),
        scratch_shapes=[
            pltpu.SemaphoreType.DMA((devices, 3)),
            pltpu.SemaphoreType.DMA((devices,)),
            pltpu.SemaphoreType.DMA((devices,)),
            pltpu.SemaphoreType.DMA((devices,)),
            pltpu.SemaphoreType.DMA((devices,)),
        ],
        compiler_params=pltpu.CompilerParams(
            collective_id=0, has_side_effects=True, vmem_limit_bytes=24 * 1024 * 1024
        ),
    )(blocks, meta)
    out = pl.pallas_call(
        functools.partial(dense_kernel, dims),
        out_shape=jax.ShapeDtypeStruct((devices, capacity, size, size), jnp.bfloat16),
        in_specs=[vmem, pl.BlockSpec(memory_space=pltpu.SMEM)],
        out_specs=vmem,
        scratch_shapes=[
            pltpu.VMEM((width, width), jnp.bfloat16),
            pltpu.VMEM((width, width), jnp.bfloat16),
            pltpu.VMEM((devices, rows, width), jnp.float32),
            pltpu.VMEM((total // 2, rows * size, 2 * size), jnp.bfloat16),
        ],
        compiler_params=pltpu.CompilerParams(vmem_limit_bytes=40 * 1024 * 1024),
    )(gathered, gathered_meta)
    return out.reshape(1, 1, devices, capacity, size, size)


def solution(mesh):
    placed = (
        P(("groups", "row", "col"), None, None, None),
        P(("groups", "row", "col"), None),
        P("depth", ("groups", "row", "col"), None, None),
    )
    small = mesh.shape["row"] * mesh.shape["col"] <= 8 and mesh.shape["col"] == 2
    return jax.shard_map(
        dense_shards if small else shards,
        mesh=mesh,
        in_specs=placed,
        out_specs=P("depth", ("groups", "row", "col"), None, None, None, None),
        check_vma=False,
    )
```

```python
import functools
import math

import jax
import jax.numpy as jnp
from jax import lax
from jax.experimental import pallas as pl
from jax.experimental.pallas import tpu as pltpu
from jax.sharding import PartitionSpec as P

HOPS = 3
MESH = pl.DeviceIdType.MESH


def passed_along(value, axis, by):
    peers = lax.axis_size(axis)
    return lax.ppermute(value, axis, [(i, (i + by) % peers) for i in range(peers)])


def product_rows(left, left_pattern, local_index, near_blocks, near_pattern, first_slot, slot_span):
    slot_count = left.shape[1]
    block_size = left.shape[2]

    def one_row(row_data):
        own_blocks, own_pattern, own_local = row_data
        used_local = lax.dynamic_slice_in_dim(own_local, first_slot, slot_span, 0)
        used_blocks = lax.dynamic_slice_in_dim(own_blocks, first_slot, slot_span, 0)
        fetched = jnp.take(near_blocks, used_local, axis=0).reshape(
            slot_span, slot_count, block_size * block_size
        )
        fetched_pattern = jnp.take(near_pattern, used_local, axis=0)
        select = (fetched_pattern[:, None, :] == own_pattern[None, :, None]).astype(jnp.bfloat16)
        aligned = jnp.einsum("kjl,klx->kjx", select, fetched, preferred_element_type=jnp.bfloat16)
        aligned = aligned.reshape(slot_span, slot_count, block_size, block_size)
        return jnp.einsum("kab,kjbc->jac", used_blocks, aligned, preferred_element_type=jnp.float32)

    return lax.map(one_row, (left, left_pattern, local_index))


def regroup(updated, targets):
    device_count = lax.axis_size(("row", "col"))
    row_count = updated.shape[0]
    half_slots = updated.shape[1]
    block_size = updated.shape[2]
    item_count = row_count * half_slots
    capacity = max(2, 3 * item_count // device_count + 1)
    flat_targets = targets.reshape(item_count)
    same_owner = flat_targets[:, None] == flat_targets[None, :]
    earlier = jnp.arange(item_count)[:, None] > jnp.arange(item_count)[None, :]
    rank_index = jnp.sum((same_owner & earlier).astype(jnp.int32), axis=1)
    destination = flat_targets * capacity + rank_index
    select = (
        jnp.arange(device_count * capacity, dtype=jnp.int32)[:, None] == destination[None, :]
    ).astype(jnp.bfloat16)
    outgoing = jnp.dot(
        select,
        updated.reshape(item_count, block_size * block_size),
        preferred_element_type=jnp.float32,
    ).astype(jnp.bfloat16)
    outgoing = outgoing.reshape(device_count, capacity, block_size, block_size)
    received = lax.all_to_all(outgoing, ("row", "col"), split_axis=0, concat_axis=0, tiled=True)
    return received.reshape(1, 1, device_count, capacity, block_size, block_size)


def shards(blocks, pattern, owner_map):
    row_count = blocks.shape[0]
    slot_count = blocks.shape[1]
    block_size = blocks.shape[2]
    half_slots = slot_count // 2
    device_count = lax.axis_size(("row", "col"))
    total_rows = device_count * row_count
    position = lax.axis_index(("row", "col"))
    layer_index = lax.axis_index("depth")
    inv_scale = 1.0 / math.sqrt(block_size * slot_count)
    targets = owner_map[0, :, :, 0]
    offsets = list(range(HOPS, 0, -1)) + list(range(-1, -HOPS - 1, -1))
    arrivals = [passed_along((blocks, pattern), ("row", "col"), offset) for offset in offsets]
    near_blocks = jnp.concatenate(
        [arrived[0] for arrived in arrivals[:HOPS]]
        + [blocks]
        + [arrived[0] for arrived in arrivals[HOPS:]],
        axis=0,
    )
    near_pattern = jnp.concatenate(
        [arrived[1] for arrived in arrivals[:HOPS]]
        + [pattern]
        + [arrived[1] for arrived in arrivals[HOPS:]],
        axis=0,
    )
    first_row = (position - HOPS) * row_count
    local_index = (pattern - first_row) % total_rows
    first_slot = layer_index * half_slots
    partial_value = product_rows(
        blocks, pattern, local_index, near_blocks, near_pattern, first_slot, half_slots
    )
    squared = (lax.psum(partial_value, "depth") * inv_scale).astype(jnp.bfloat16)
    w_arrivals = [passed_along(squared, ("row", "col"), offset) for offset in offsets]
    near_squared = jnp.concatenate(w_arrivals[:HOPS] + [squared] + w_arrivals[HOPS:], axis=0)
    partial_value = product_rows(
        blocks, pattern, local_index, near_squared, near_pattern, first_slot, half_slots
    )
    cubic_term = lax.psum_scatter(
        partial_value.astype(jnp.bfloat16), "depth", scatter_dimension=1, tiled=True
    ).astype(jnp.float32)
    own_blocks = lax.dynamic_slice_in_dim(blocks, first_slot, half_slots, 1)
    updated = (1.5 * own_blocks.astype(jnp.float32) - 0.5 * inv_scale * cubic_term).astype(
        jnp.bfloat16
    )
    return regroup(updated, targets)


def gather_kernel(
    dims, blocks_ref, meta_ref, packed, meta_v,
    send_sem, recv_sem, sib_sem, meta_send, meta_recv,
):
    n_row, n_col, rows, slots, size, capacity = dims
    devices = n_row * n_col
    part = rows * size
    half_rows = slots // 2 * size
    z, x, h = lax.axis_index("row"), lax.axis_index("col"), lax.axis_index("depth")
    me = z * n_col + x
    across = n_col - 1 - x

    def device(to_z, to_x, to_h):
        return {"row": to_z, "col": to_x, "depth": to_h}

    sibling = device(z, x, 1 - h)

    barrier = pltpu.get_barrier_semaphore()
    for step in range(1, devices):
        peer = lax.rem(me + step, devices)
        pl.semaphore_signal(
            barrier, inc=1, device_id=device(peer // n_col, lax.rem(peer, n_col), h),
            device_id_type=MESH,
        )
    pl.semaphore_signal(barrier, inc=1, device_id=sibling, device_id_type=MESH)

    for pair in range(rows // 2):
        packed[me, : slots * size, pair * 2 * size : (pair + 1) * 2 * size] = jnp.concatenate(
            [blocks_ref[2 * pair + t].reshape(slots * size, size) for t in range(2)], axis=1
        )
    for source in range(devices):
        packed[source, slots * size :, :] = jnp.zeros((size, part), jnp.bfloat16)
    meta_v[me] = meta_ref[...]
    pl.semaphore_wait(barrier, devices)

    def meta_copy(step):
        peer = lax.rem(me + step, devices)
        return pltpu.make_async_remote_copy(
            src_ref=meta_v.at[me], dst_ref=meta_v.at[me],
            send_sem=meta_send.at[step], recv_sem=meta_recv.at[step],
            device_id=device(peer // n_col, lax.rem(peer, n_col), h), device_id_type=MESH,
        )

    def piece(position, which):
        return packed.at[position, pl.ds(which * half_rows, half_rows), :]

    def copy(position, k, target, landed, which=None):
        ref = piece(position, h if which is None else which)
        return pltpu.make_async_remote_copy(
            src_ref=ref, dst_ref=ref, send_sem=send_sem.at[position, k],
            recv_sem=landed.at[position], device_id=target, device_id_type=MESH,
        )

    sends = []

    def start(valid, position, k, target, landed):
        @pl.when(valid)
        def _():
            copy(position, k, target, landed).start()
        sends.append((valid, position, k, target, landed))

    for step in range(1, devices):
        meta_copy(step).start()
    start(z > 0, me, 0, device(z - 1, x, h), recv_sem)
    start(z < n_row - 1, me, 1, device(z + 1, x, h), recv_sem)
    start(z >= 0, me, 2, device(z, across, h), recv_sem)

    def from_z(distance, way):
        source = z + way * distance
        valid = (source >= 0) & (source < n_row)
        position = source * n_col + x

        @pl.when(valid)
        def _():
            copy(position, 0, sibling, recv_sem).wait_recv()
        start(valid & (z - way >= 0) & (z - way < n_row), position, 0, device(z - way, x, h), recv_sem)
        start(valid, position, 1, device(z, across, h), recv_sem)
        start(valid, position, 2, sibling, sib_sem)

    def from_x(distance, way):
        source = z + way * distance
        valid = (source >= 0) & (source < n_row)
        position = source * n_col + across

        @pl.when(valid)
        def _():
            copy(position, 0, sibling, recv_sem).wait_recv()
        start(valid, position, 0, sibling, sib_sem)

    for distance in range(1, n_row):
        from_z(distance, 1)
        from_z(distance, -1)
        if distance == 1:
            from_x(0, 1)
        else:
            from_x(distance - 1, 1)
            from_x(distance - 1, -1)
    from_x(n_row - 1, 1)
    from_x(n_row - 1, -1)

    for step in range(1, devices):
        meta_copy(step).wait()
    for step in range(1, devices):
        position = lax.rem(me + step, devices)
        copy(position, 0, sibling, sib_sem, 1 - h).wait_recv()
    for valid, position, k, target, landed in sends:
        @pl.when(valid)
        def _(position=position, k=k, target=target, landed=landed):
            copy(position, k, target, landed).wait_send()


def chunk_product(devices, part, left_ref, right_ref, source, d):
    def chunk(r):
        return pl.ds(pl.multiple_of(lax.rem(source + r + devices, devices) * part, part), part)

    def apart(r):
        return min(r % devices, -r % devices)

    between = [r for r in range(-HOPS, HOPS + 1) if apart(r - d) <= HOPS]
    left = jnp.concatenate([left_ref[chunk(0), chunk(r)] for r in between], axis=1)
    right = jnp.concatenate([right_ref[chunk(r), chunk(d)] for r in between], axis=0)
    return chunk(0), chunk(d), jnp.dot(left, right, preferred_element_type=jnp.float32)


def dense_kernel(dims, packed, meta_s, out_ref, x_ref, sq_ref, mask_ref, up_ref):
    n_row, n_col, rows, slots, size, capacity = dims
    devices = n_row * n_col
    total = devices * rows
    width = total * size
    part = rows * size
    me = lax.axis_index("row") * n_col + lax.axis_index("col")

    lane = lax.broadcasted_iota(jnp.int32, (1, 2 * size), 1)

    def expand(source, carry):
        for row in range(rows):
            lanes = row // 2 * 2 * size
            at = row % 2 * size
            for pair in range(total // 2):
                slot = [meta_s[source, 0, row * total + 2 * pair + t] for t in range(2)]
                both = [
                    packed[source, pl.ds(pl.multiple_of(slot[t] * size, size), size), lanes : lanes + 2 * size]
                    for t in range(2)
                ]
                spot = slice(pair * 2 * size, (pair + 1) * 2 * size)
                x_ref[pl.ds(pl.multiple_of(source * part + row * size, size), size), spot] = (
                    jnp.concatenate([both[t][:, at : at + size] for t in range(2)], axis=1)
                )
                kept = [(slot[t] < slots).astype(jnp.float32) for t in range(2)]
                mask_ref[source, row : row + 1, spot] = jnp.where(lane < size, kept[0], kept[1])
        return carry

    lax.fori_loop(0, devices, expand, 0)

    inv_scale = 1.0 / math.sqrt(size * slots)

    def square(source, carry):
        for d in range(-HOPS, HOPS + 1):
            own, spot, value = chunk_product(devices, part, x_ref, x_ref, source, d)
            kept = jnp.broadcast_to(mask_ref[source, :, spot][:, None, :], (rows, size, part))
            sq_ref[own, spot] = (value * inv_scale * kept.reshape(part, part)).astype(jnp.bfloat16)
        return carry

    lax.fori_loop(0, devices, square, 0)

    def cube(source, carry):
        for d in range(-HOPS, HOPS + 1):
            own, spot, value = chunk_product(devices, part, x_ref, sq_ref, source, d)
            value = 1.5 * x_ref[own, spot].astype(jnp.float32) - (0.5 * inv_scale) * value
            value = value.astype(jnp.bfloat16)
            column = lax.rem(source + d + devices, devices)
            for t in range(rows // 2):
                up_ref[column * (rows // 2) + t] = value[:, t * 2 * size : (t + 1) * 2 * size]
        for rank in range(capacity):
            code = meta_s[source, 1, me * capacity + rank]
            found = jnp.maximum(code, 0)
            column = found & (total - 1)
            row = found >> (total.bit_length() - 1)
            block = up_ref[column >> 1, pl.ds(pl.multiple_of(row * size, size), size), :]
            block = block.astype(jnp.float32)
            block = jnp.where((column & 1) == 0, block[:, :size], block[:, size:])
            out_ref[source, rank] = jnp.where(code >= 0, block, 0.0).astype(jnp.bfloat16)
        return carry

    lax.fori_loop(0, devices, cube, 0)


def dense_shards(blocks, pattern, owner_map):
    rows, slots, size, _ = blocks.shape
    n_row, n_col = lax.axis_size("row"), lax.axis_size("col")
    devices = n_row * n_col
    total = devices * rows
    items = rows * (slots // 2)
    capacity = max(2, 3 * items // devices + 1)
    h = lax.axis_index("depth")

    slot_number = jnp.arange(slots, dtype=jnp.int32)[None, :, None]
    named = pattern[:, :, None] == jnp.arange(total, dtype=jnp.int32)[None, None, :]
    slot_of = slots + jnp.sum(jnp.where(named, slot_number - slots, 0), axis=1)

    targets = owner_map.reshape(items)
    earlier = jnp.arange(items)[:, None] > jnp.arange(items)[None, :]
    rank = jnp.sum(((targets[:, None] == targets[None, :]) & earlier).astype(jnp.int32), axis=1)
    columns = lax.dynamic_slice_in_dim(pattern, h * (slots // 2), slots // 2, 1)
    code = jnp.arange(rows, dtype=jnp.int32)[:, None] * total + columns
    placed = jnp.arange(devices * capacity, dtype=jnp.int32)[:, None] == (targets * capacity + rank)[None, :]
    item_at = jnp.sum(jnp.where(placed, code.reshape(1, items) + 1, 0), axis=1) - 1
    lanes = 128
    meta = jnp.concatenate(
        [slot_of.reshape(1, lanes), item_at.reshape(1, lanes), jnp.zeros((6, lanes), jnp.int32)], axis=0
    )
    dims = (n_row, n_col, rows, slots, size, capacity)
    width = total * size
    vmem = pl.BlockSpec(memory_space=pltpu.VMEM)
    gathered, gathered_meta = pl.pallas_call(
        functools.partial(gather_kernel, dims),
        out_shape=(
            jax.ShapeDtypeStruct((devices, (slots + 1) * size, rows * size), jnp.bfloat16),
            jax.ShapeDtypeStruct((devices, 8, lanes), jnp.int32),
        ),
        in_specs=[vmem, vmem],
        out_specs=(vmem, vmem),
        scratch_shapes=[
            pltpu.SemaphoreType.DMA((devices, 3)),
            pltpu.SemaphoreType.DMA((devices,)),
            pltpu.SemaphoreType.DMA((devices,)),
            pltpu.SemaphoreType.DMA((devices,)),
            pltpu.SemaphoreType.DMA((devices,)),
        ],
        compiler_params=pltpu.CompilerParams(
            collective_id=0, has_side_effects=True, vmem_limit_bytes=24 * 1024 * 1024
        ),
    )(blocks, meta)
    out = pl.pallas_call(
        functools.partial(dense_kernel, dims),
        out_shape=jax.ShapeDtypeStruct((devices, capacity, size, size), jnp.bfloat16),
        in_specs=[vmem, pl.BlockSpec(memory_space=pltpu.SMEM)],
        out_specs=vmem,
        scratch_shapes=[
            pltpu.VMEM((width, width), jnp.bfloat16),
            pltpu.VMEM((width, width), jnp.bfloat16),
            pltpu.VMEM((devices, rows, width), jnp.float32),
            pltpu.VMEM((total // 2, rows * size, 2 * size), jnp.bfloat16),
        ],
        compiler_params=pltpu.CompilerParams(vmem_limit_bytes=40 * 1024 * 1024),
    )(gathered, gathered_meta)
    return out.reshape(1, 1, devices, capacity, size, size)


def solution(mesh):
    placed = (
        P(("groups", "row", "col"), None, None, None),
        P(("groups", "row", "col"), None),
        P("depth", ("groups", "row", "col"), None, None),
    )
    small = mesh.shape["row"] * mesh.shape["col"] == 8 and mesh.shape["col"] == 2
    return jax.shard_map(
        dense_shards if small else shards,
        mesh=mesh,
        in_specs=placed,
        out_specs=P("depth", ("groups", "row", "col"), None, None, None, None),
        check_vma=False,
    )
```

```python
import functools
import math

import jax
import jax.numpy as jnp
from jax import lax
from jax.experimental import pallas as pl
from jax.experimental.pallas import tpu as pltpu
from jax.sharding import PartitionSpec as P

HOPS = 3
MESH = pl.DeviceIdType.MESH


def passed_along(value, axis, by):
    peers = lax.axis_size(axis)
    return lax.ppermute(value, axis, [(i, (i + by) % peers) for i in range(peers)])


def product_rows(left, left_pattern, local_index, near_blocks, near_pattern, first_slot, slot_span):
    slot_count = left.shape[1]
    block_size = left.shape[2]

    def one_row(row_data):
        own_blocks, own_pattern, own_local = row_data
        used_local = lax.dynamic_slice_in_dim(own_local, first_slot, slot_span, 0)
        used_blocks = lax.dynamic_slice_in_dim(own_blocks, first_slot, slot_span, 0)
        fetched = jnp.take(near_blocks, used_local, axis=0).reshape(
            slot_span, slot_count, block_size * block_size
        )
        fetched_pattern = jnp.take(near_pattern, used_local, axis=0)
        select = (fetched_pattern[:, None, :] == own_pattern[None, :, None]).astype(jnp.bfloat16)
        aligned = jnp.einsum("kjl,klx->kjx", select, fetched, preferred_element_type=jnp.bfloat16)
        aligned = aligned.reshape(slot_span, slot_count, block_size, block_size)
        return jnp.einsum("kab,kjbc->jac", used_blocks, aligned, preferred_element_type=jnp.float32)

    return lax.map(one_row, (left, left_pattern, local_index))


def regroup(updated, targets):
    device_count = lax.axis_size(("row", "col"))
    row_count = updated.shape[0]
    half_slots = updated.shape[1]
    block_size = updated.shape[2]
    item_count = row_count * half_slots
    capacity = max(2, 3 * item_count // device_count + 1)
    flat_targets = targets.reshape(item_count)
    same_owner = flat_targets[:, None] == flat_targets[None, :]
    earlier = jnp.arange(item_count)[:, None] > jnp.arange(item_count)[None, :]
    rank_index = jnp.sum((same_owner & earlier).astype(jnp.int32), axis=1)
    destination = flat_targets * capacity + rank_index
    select = (
        jnp.arange(device_count * capacity, dtype=jnp.int32)[:, None] == destination[None, :]
    ).astype(jnp.bfloat16)
    outgoing = jnp.dot(
        select,
        updated.reshape(item_count, block_size * block_size),
        preferred_element_type=jnp.float32,
    ).astype(jnp.bfloat16)
    outgoing = outgoing.reshape(device_count, capacity, block_size, block_size)
    received = lax.all_to_all(outgoing, ("row", "col"), split_axis=0, concat_axis=0, tiled=True)
    return received.reshape(1, 1, device_count, capacity, block_size, block_size)


def shards(blocks, pattern, owner_map):
    row_count = blocks.shape[0]
    slot_count = blocks.shape[1]
    block_size = blocks.shape[2]
    half_slots = slot_count // 2
    device_count = lax.axis_size(("row", "col"))
    total_rows = device_count * row_count
    position = lax.axis_index(("row", "col"))
    layer_index = lax.axis_index("depth")
    inv_scale = 1.0 / math.sqrt(block_size * slot_count)
    targets = owner_map[0, :, :, 0]
    offsets = list(range(HOPS, 0, -1)) + list(range(-1, -HOPS - 1, -1))
    arrivals = [passed_along((blocks, pattern), ("row", "col"), offset) for offset in offsets]
    near_blocks = jnp.concatenate(
        [arrived[0] for arrived in arrivals[:HOPS]]
        + [blocks]
        + [arrived[0] for arrived in arrivals[HOPS:]],
        axis=0,
    )
    near_pattern = jnp.concatenate(
        [arrived[1] for arrived in arrivals[:HOPS]]
        + [pattern]
        + [arrived[1] for arrived in arrivals[HOPS:]],
        axis=0,
    )
    first_row = (position - HOPS) * row_count
    local_index = (pattern - first_row) % total_rows
    first_slot = layer_index * half_slots
    partial_value = product_rows(
        blocks, pattern, local_index, near_blocks, near_pattern, first_slot, half_slots
    )
    squared = (lax.psum(partial_value, "depth") * inv_scale).astype(jnp.bfloat16)
    w_arrivals = [passed_along(squared, ("row", "col"), offset) for offset in offsets]
    near_squared = jnp.concatenate(w_arrivals[:HOPS] + [squared] + w_arrivals[HOPS:], axis=0)
    partial_value = product_rows(
        blocks, pattern, local_index, near_squared, near_pattern, first_slot, half_slots
    )
    cubic_term = lax.psum_scatter(
        partial_value.astype(jnp.bfloat16), "depth", scatter_dimension=1, tiled=True
    ).astype(jnp.float32)
    own_blocks = lax.dynamic_slice_in_dim(blocks, first_slot, half_slots, 1)
    updated = (1.5 * own_blocks.astype(jnp.float32) - 0.5 * inv_scale * cubic_term).astype(
        jnp.bfloat16
    )
    return regroup(updated, targets)


def gather_kernel(
    dims, blocks_ref, meta_ref, x_ref, sq_ref, meta_v,
    packed, meta_s, mask_ref,
    send_sem, recv_sem, sib_sem, meta_send, meta_recv, local_sem, sq_send, sq_recv,
):
    n_row, n_col, rows, slots, size, capacity = dims
    devices = n_row * n_col
    total = devices * rows
    part = rows * size
    half_slots = slots // 2
    z, x, h = lax.axis_index("row"), lax.axis_index("col"), lax.axis_index("depth")
    me = z * n_col + x
    across = n_col - 1 - x

    def device(to_z, to_x, to_h):
        return {"row": to_z, "col": to_x, "depth": to_h}

    sibling = device(z, x, 1 - h)

    barrier = pltpu.get_barrier_semaphore()
    for step in range(1, devices):
        peer = lax.rem(me + step, devices)
        pl.semaphore_signal(
            barrier, inc=1, device_id=device(peer // n_col, lax.rem(peer, n_col), h),
            device_id_type=MESH,
        )
    pl.semaphore_signal(barrier, inc=1, device_id=sibling, device_id_type=MESH)

    for pair in range(rows // 2):
        packed[me, :slots, :, pair * 2 * size : (pair + 1) * 2 * size] = jnp.concatenate(
            [blocks_ref[2 * pair + t] for t in range(2)], axis=2
        )
    for source in range(devices):
        packed[source, slots] = jnp.zeros((size, part), jnp.bfloat16)
    meta_v[me] = meta_ref[...]
    pl.semaphore_wait(barrier, devices)

    def meta_copy(step):
        peer = lax.rem(me + step, devices)
        return pltpu.make_async_remote_copy(
            src_ref=meta_v.at[me], dst_ref=meta_v.at[me],
            send_sem=meta_send.at[step], recv_sem=meta_recv.at[step],
            device_id=device(peer // n_col, lax.rem(peer, n_col), h), device_id_type=MESH,
        )

    def piece(position, which):
        return packed.at[position, pl.ds(which * half_slots, half_slots)]

    def copy(position, k, target, landed, which=None):
        ref = piece(position, h if which is None else which)
        return pltpu.make_async_remote_copy(
            src_ref=ref, dst_ref=ref, send_sem=send_sem.at[position, k],
            recv_sem=landed.at[position], device_id=target, device_id_type=MESH,
        )

    sends = []

    def start(valid, position, k, target, landed):
        @pl.when(valid)
        def _():
            copy(position, k, target, landed).start()
        sends.append((valid, position, k, target, landed))

    for step in range(1, devices):
        meta_copy(step).start()
    start(z > 0, me, 0, device(z - 1, x, h), recv_sem)
    start(z < n_row - 1, me, 1, device(z + 1, x, h), recv_sem)
    start(z >= 0, me, 2, device(z, across, h), recv_sem)

    def from_z(distance, way):
        source = z + way * distance
        valid = (source >= 0) & (source < n_row)
        position = source * n_col + x

        @pl.when(valid)
        def _():
            copy(position, 0, sibling, recv_sem).wait_recv()
        start(valid & (z - way >= 0) & (z - way < n_row), position, 0, device(z - way, x, h), recv_sem)
        start(valid, position, 1, device(z, across, h), recv_sem)
        start(valid, position, 2, sibling, sib_sem)

    def from_x(distance, way):
        source = z + way * distance
        valid = (source >= 0) & (source < n_row)
        position = source * n_col + across

        @pl.when(valid)
        def _():
            copy(position, 0, sibling, recv_sem).wait_recv()
        start(valid, position, 0, sibling, sib_sem)

    for distance in range(1, n_row):
        from_z(distance, 1)
        from_z(distance, -1)
        if distance == 1:
            from_x(0, 1)
        else:
            from_x(distance - 1, 1)
            from_x(distance - 1, -1)
    from_x(n_row - 1, 1)
    from_x(n_row - 1, -1)

    for step in range(1, devices):
        meta_copy(step).wait()
    local = pltpu.make_async_copy(meta_v, meta_s, local_sem)
    local.start()
    local.wait()
    for step in range(1, devices):
        position = lax.rem(me + step, devices)
        copy(position, 0, sibling, sib_sem, 1 - h).wait_recv()
    for valid, position, k, target, landed in sends:
        @pl.when(valid)
        def _(position=position, k=k, target=target, landed=landed):
            copy(position, k, target, landed).wait_send()

    lane = lax.broadcasted_iota(jnp.int32, (1, 2 * size), 1)

    def expand(source, carry):
        for row in range(rows):
            lanes = row // 2 * 2 * size
            at = row % 2 * size
            for pair in range(total // 2):
                slot = [meta_s[source, 0, row * total + 2 * pair + t] for t in range(2)]
                both = [
                    packed[source, slot[t], :, lanes : lanes + 2 * size]
                    for t in range(2)
                ]
                spot = slice(pair * 2 * size, (pair + 1) * 2 * size)
                x_ref[pl.ds(pl.multiple_of(source * part + row * size, size), size), spot] = (
                    jnp.concatenate([both[t][:, at : at + size] for t in range(2)], axis=1)
                )
                kept = [(slot[t] < slots).astype(jnp.float32) for t in range(2)]
                mask_ref[source, row : row + 1, spot] = jnp.where(lane < size, kept[0], kept[1])
        return carry

    lax.fori_loop(0, devices, expand, 0)

    inv_scale = 1.0 / math.sqrt(size * slots)
    share = devices // 2

    def half_copy(side, step):
        ref = sq_ref.at[pl.ds((side * share + step) * part, part), :]
        return pltpu.make_async_remote_copy(
            src_ref=ref, dst_ref=ref, send_sem=sq_send.at[step], recv_sem=sq_recv.at[step],
            device_id=sibling, device_id_type=MESH,
        )

    def square(step, carry):
        source = h * share + step
        for d in range(-HOPS, HOPS + 1):
            own, spot, value = chunk_product(devices, part, x_ref, x_ref, source, d)
            kept = jnp.broadcast_to(mask_ref[source, :, spot][:, None, :], (rows, size, part))
            sq_ref[own, spot] = (value * inv_scale * kept.reshape(part, part)).astype(jnp.bfloat16)
        far = pl.ds(pl.multiple_of(lax.rem(source + HOPS + 1, devices) * part, part), part)
        sq_ref[own, far] = jnp.zeros((part, part), jnp.bfloat16)
        half_copy(h, step).start()
        return carry

    lax.fori_loop(0, share, square, 0)
    for step in range(share):
        half_copy(h, step).wait_send()
        half_copy(1 - h, step).wait_recv()


def chunk_product(devices, part, left_ref, right_ref, source, d):
    def chunk(r):
        return pl.ds(pl.multiple_of(lax.rem(source + r + devices, devices) * part, part), part)

    def apart(r):
        return min(r % devices, -r % devices)

    between = [r for r in range(-HOPS, HOPS + 1) if apart(r - d) <= HOPS]
    left = jnp.concatenate([left_ref[chunk(0), chunk(r)] for r in between], axis=1)
    right = jnp.concatenate([right_ref[chunk(r), chunk(d)] for r in between], axis=0)
    return chunk(0), chunk(d), jnp.dot(left, right, preferred_element_type=jnp.float32)


def dense_kernel(dims, x_ref, sq_ref, meta_s, out_ref, up_ref):
    n_row, n_col, rows, slots, size, capacity = dims
    devices = n_row * n_col
    total = devices * rows
    width = total * size
    part = rows * size
    me = lax.axis_index("row") * n_col + lax.axis_index("col")

    inv_scale = 1.0 / math.sqrt(size * slots)

    def cube(source, carry):
        for d in range(-HOPS, HOPS + 1):
            own, spot, value = chunk_product(devices, part, x_ref, sq_ref, source, d)
            value = 1.5 * x_ref[own, spot].astype(jnp.float32) - (0.5 * inv_scale) * value
            value = value.astype(jnp.bfloat16)
            column = lax.rem(source + d + devices, devices)
            for t in range(rows // 2):
                up_ref[column * (rows // 2) + t] = value[:, t * 2 * size : (t + 1) * 2 * size]
        for rank in range(capacity):
            code = meta_s[source, 1, me * capacity + rank]
            found = jnp.maximum(code, 0)
            column = found & (total - 1)
            row = found >> (total.bit_length() - 1)
            block = up_ref[column >> 1, pl.ds(pl.multiple_of(row * size, size), size), :]
            block = block.astype(jnp.float32)
            block = jnp.where((column & 1) == 0, block[:, :size], block[:, size:])
            out_ref[source, rank] = jnp.where(code >= 0, block, 0.0).astype(jnp.bfloat16)
        return carry

    lax.fori_loop(0, devices, cube, 0)


def dense_shards(blocks, pattern, owner_map):
    rows, slots, size, _ = blocks.shape
    n_row, n_col = lax.axis_size("row"), lax.axis_size("col")
    devices = n_row * n_col
    total = devices * rows
    items = rows * (slots // 2)
    capacity = max(2, 3 * items // devices + 1)
    h = lax.axis_index("depth")

    slot_number = jnp.arange(slots, dtype=jnp.int32)[None, :, None]
    named = pattern[:, :, None] == jnp.arange(total, dtype=jnp.int32)[None, None, :]
    slot_of = slots + jnp.sum(jnp.where(named, slot_number - slots, 0), axis=1)

    targets = owner_map.reshape(items)
    earlier = jnp.arange(items)[:, None] > jnp.arange(items)[None, :]
    rank = jnp.sum(((targets[:, None] == targets[None, :]) & earlier).astype(jnp.int32), axis=1)
    columns = lax.dynamic_slice_in_dim(pattern, h * (slots // 2), slots // 2, 1)
    code = jnp.arange(rows, dtype=jnp.int32)[:, None] * total + columns
    placed = jnp.arange(devices * capacity, dtype=jnp.int32)[:, None] == (targets * capacity + rank)[None, :]
    item_at = jnp.sum(jnp.where(placed, code.reshape(1, items) + 1, 0), axis=1) - 1
    lanes = 128
    meta = jnp.concatenate(
        [slot_of.reshape(1, lanes), item_at.reshape(1, lanes), jnp.zeros((6, lanes), jnp.int32)], axis=0
    )
    dims = (n_row, n_col, rows, slots, size, capacity)
    width = total * size
    vmem = pl.BlockSpec(memory_space=pltpu.VMEM)
    dense, squared, gathered_meta = pl.pallas_call(
        functools.partial(gather_kernel, dims),
        out_shape=(
            jax.ShapeDtypeStruct((width, width), jnp.bfloat16),
            jax.ShapeDtypeStruct((width, width), jnp.bfloat16),
            jax.ShapeDtypeStruct((devices, 8, lanes), jnp.int32),
        ),
        in_specs=[vmem, vmem],
        out_specs=(vmem, vmem, vmem),
        scratch_shapes=[
            pltpu.VMEM((devices, slots + 1, size, rows * size), jnp.bfloat16),
            pltpu.SMEM((devices, 8, lanes), jnp.int32),
            pltpu.VMEM((devices, rows, width), jnp.float32),
            pltpu.SemaphoreType.DMA((devices, 3)),
            pltpu.SemaphoreType.DMA((devices,)),
            pltpu.SemaphoreType.DMA((devices,)),
            pltpu.SemaphoreType.DMA((devices,)),
            pltpu.SemaphoreType.DMA((devices,)),
            pltpu.SemaphoreType.DMA,
            pltpu.SemaphoreType.DMA((devices // 2,)),
            pltpu.SemaphoreType.DMA((devices // 2,)),
        ],
        compiler_params=pltpu.CompilerParams(
            collective_id=0, has_side_effects=True, vmem_limit_bytes=32 * 1024 * 1024
        ),
    )(blocks, meta)
    out = pl.pallas_call(
        functools.partial(dense_kernel, dims),
        out_shape=jax.ShapeDtypeStruct((devices, capacity, size, size), jnp.bfloat16),
        in_specs=[vmem, vmem, pl.BlockSpec(memory_space=pltpu.SMEM)],
        out_specs=vmem,
        scratch_shapes=[pltpu.VMEM((total // 2, rows * size, 2 * size), jnp.bfloat16)],
        compiler_params=pltpu.CompilerParams(vmem_limit_bytes=28 * 1024 * 1024),
    )(dense, squared, gathered_meta)
    return out.reshape(1, 1, devices, capacity, size, size)


def solution(mesh):
    placed = (
        P(("groups", "row", "col"), None, None, None),
        P(("groups", "row", "col"), None),
        P("depth", ("groups", "row", "col"), None, None),
    )
    small = mesh.shape["row"] * mesh.shape["col"] == 8 and mesh.shape["col"] == 2
    return jax.shard_map(
        dense_shards if small else shards,
        mesh=mesh,
        in_specs=placed,
        out_specs=P("depth", ("groups", "row", "col"), None, None, None, None),
        check_vma=False,
    )
```

```python
import functools
import math

import jax
import jax.numpy as jnp
from jax import lax
from jax.experimental import pallas as pl
from jax.experimental.pallas import tpu as pltpu
from jax.sharding import PartitionSpec as P

HOPS = 3
MESH = pl.DeviceIdType.MESH


def passed_along(value, axis, by):
    peers = lax.axis_size(axis)
    return lax.ppermute(value, axis, [(i, (i + by) % peers) for i in range(peers)])


def product_rows(left, left_pattern, local_index, near_blocks, near_pattern, first_slot, slot_span):
    slot_count = left.shape[1]
    block_size = left.shape[2]

    def one_row(row_data):
        own_blocks, own_pattern, own_local = row_data
        used_local = lax.dynamic_slice_in_dim(own_local, first_slot, slot_span, 0)
        used_blocks = lax.dynamic_slice_in_dim(own_blocks, first_slot, slot_span, 0)
        fetched = jnp.take(near_blocks, used_local, axis=0).reshape(
            slot_span, slot_count, block_size * block_size
        )
        fetched_pattern = jnp.take(near_pattern, used_local, axis=0)
        select = (fetched_pattern[:, None, :] == own_pattern[None, :, None]).astype(jnp.bfloat16)
        aligned = jnp.einsum("kjl,klx->kjx", select, fetched, preferred_element_type=jnp.bfloat16)
        aligned = aligned.reshape(slot_span, slot_count, block_size, block_size)
        return jnp.einsum("kab,kjbc->jac", used_blocks, aligned, preferred_element_type=jnp.float32)

    return lax.map(one_row, (left, left_pattern, local_index))


def regroup(updated, targets):
    device_count = lax.axis_size(("row", "col"))
    row_count = updated.shape[0]
    half_slots = updated.shape[1]
    block_size = updated.shape[2]
    item_count = row_count * half_slots
    capacity = max(2, 3 * item_count // device_count + 1)
    flat_targets = targets.reshape(item_count)
    same_owner = flat_targets[:, None] == flat_targets[None, :]
    earlier = jnp.arange(item_count)[:, None] > jnp.arange(item_count)[None, :]
    rank_index = jnp.sum((same_owner & earlier).astype(jnp.int32), axis=1)
    destination = flat_targets * capacity + rank_index
    select = (
        jnp.arange(device_count * capacity, dtype=jnp.int32)[:, None] == destination[None, :]
    ).astype(jnp.bfloat16)
    outgoing = jnp.dot(
        select,
        updated.reshape(item_count, block_size * block_size),
        preferred_element_type=jnp.float32,
    ).astype(jnp.bfloat16)
    outgoing = outgoing.reshape(device_count, capacity, block_size, block_size)
    received = lax.all_to_all(outgoing, ("row", "col"), split_axis=0, concat_axis=0, tiled=True)
    return received.reshape(1, 1, device_count, capacity, block_size, block_size)


def shards(blocks, pattern, owner_map):
    row_count = blocks.shape[0]
    slot_count = blocks.shape[1]
    block_size = blocks.shape[2]
    half_slots = slot_count // 2
    device_count = lax.axis_size(("row", "col"))
    total_rows = device_count * row_count
    position = lax.axis_index(("row", "col"))
    layer_index = lax.axis_index("depth")
    inv_scale = 1.0 / math.sqrt(block_size * slot_count)
    targets = owner_map[0, :, :, 0]
    offsets = list(range(HOPS, 0, -1)) + list(range(-1, -HOPS - 1, -1))
    arrivals = [passed_along((blocks, pattern), ("row", "col"), offset) for offset in offsets]
    near_blocks = jnp.concatenate(
        [arrived[0] for arrived in arrivals[:HOPS]]
        + [blocks]
        + [arrived[0] for arrived in arrivals[HOPS:]],
        axis=0,
    )
    near_pattern = jnp.concatenate(
        [arrived[1] for arrived in arrivals[:HOPS]]
        + [pattern]
        + [arrived[1] for arrived in arrivals[HOPS:]],
        axis=0,
    )
    first_row = (position - HOPS) * row_count
    local_index = (pattern - first_row) % total_rows
    first_slot = layer_index * half_slots
    partial_value = product_rows(
        blocks, pattern, local_index, near_blocks, near_pattern, first_slot, half_slots
    )
    squared = (lax.psum(partial_value, "depth") * inv_scale).astype(jnp.bfloat16)
    w_arrivals = [passed_along(squared, ("row", "col"), offset) for offset in offsets]
    near_squared = jnp.concatenate(w_arrivals[:HOPS] + [squared] + w_arrivals[HOPS:], axis=0)
    partial_value = product_rows(
        blocks, pattern, local_index, near_squared, near_pattern, first_slot, half_slots
    )
    cubic_term = lax.psum_scatter(
        partial_value.astype(jnp.bfloat16), "depth", scatter_dimension=1, tiled=True
    ).astype(jnp.float32)
    own_blocks = lax.dynamic_slice_in_dim(blocks, first_slot, half_slots, 1)
    updated = (1.5 * own_blocks.astype(jnp.float32) - 0.5 * inv_scale * cubic_term).astype(
        jnp.bfloat16
    )
    return regroup(updated, targets)


def gather_kernel(
    dims, blocks_hbm, pattern_ref, owner_ref, x_ref, sq_ref, meta_v,
    blocks_ref, packed, meta_s, mask_ref,
    send_sem, recv_sem, sib_sem, meta_send, meta_recv, local_sem, sq_send, sq_recv, load_sem,
):
    n_row, n_col, rows, slots, size, capacity = dims
    devices = n_row * n_col
    total = devices * rows
    part = rows * size
    lanes = meta_v.shape[2]
    half_slots = slots // 2
    z, x, h = lax.axis_index("row"), lax.axis_index("col"), lax.axis_index("depth")
    me = z * n_col + x
    across = n_col - 1 - x

    def device(to_z, to_x, to_h):
        return {"row": to_z, "col": to_x, "depth": to_h}

    sibling = device(z, x, 1 - h)
    load = pltpu.make_async_copy(blocks_hbm, blocks_ref, load_sem)
    load.start()

    barrier = pltpu.get_barrier_semaphore()
    for step in range(1, devices):
        peer = lax.rem(me + step, devices)
        pl.semaphore_signal(
            barrier, inc=1, device_id=device(peer // n_col, lax.rem(peer, n_col), h),
            device_id_type=MESH,
        )
    pl.semaphore_signal(barrier, inc=1, device_id=sibling, device_id_type=MESH)

    for source in range(devices):
        packed[source, slots] = jnp.zeros((size, part), jnp.bfloat16)
    load.wait()
    for pair in range(rows // 2):
        packed[me, :slots, :, pair * 2 * size : (pair + 1) * 2 * size] = jnp.concatenate(
            [blocks_ref[2 * pair + t] for t in range(2)], axis=2
        )
    pl.semaphore_wait(barrier, devices)

    def meta_copy(step):
        peer = lax.rem(me + step, devices)
        return pltpu.make_async_remote_copy(
            src_ref=meta_v.at[me], dst_ref=meta_v.at[me],
            send_sem=meta_send.at[step], recv_sem=meta_recv.at[step],
            device_id=device(peer // n_col, lax.rem(peer, n_col), h), device_id_type=MESH,
        )

    def piece(position, which):
        return packed.at[position, pl.ds(which * half_slots, half_slots)]

    def copy(position, k, target, landed, which=None):
        ref = piece(position, h if which is None else which)
        return pltpu.make_async_remote_copy(
            src_ref=ref, dst_ref=ref, send_sem=send_sem.at[position, k],
            recv_sem=landed.at[position], device_id=target, device_id_type=MESH,
        )

    sends = []

    def start(valid, position, k, target, landed):
        @pl.when(valid)
        def _():
            copy(position, k, target, landed).start()
        sends.append((valid, position, k, target, landed))

    start(z > 0, me, 0, device(z - 1, x, h), recv_sem)
    start(z < n_row - 1, me, 1, device(z + 1, x, h), recv_sem)
    start(z >= 0, me, 2, device(z, across, h), recv_sem)

    lane_number = lax.broadcasted_iota(jnp.int32, (rows, lanes), 1)
    slot_of = jnp.full((rows, lanes), slots, jnp.int32)
    for slot in range(slots):
        slot_of = jnp.where(pattern_ref[:, slot : slot + 1] == lane_number, slot, slot_of)
    meta_v[me, :rows, :] = slot_of
    meta_v[me, rows:8, :] = jnp.full((8 - rows, lanes), slots, jnp.int32)
    rank_number = lax.broadcasted_iota(jnp.int32, (devices, lanes), 1)
    owner_number = lax.broadcasted_iota(jnp.int32, (devices, lanes), 0)
    item_at = jnp.full((devices, lanes), -1, jnp.int32)
    count = jnp.zeros((devices, lanes), jnp.int32)
    for row in range(rows):
        for slot in range(half_slots):
            named = owner_number == owner_ref[row, :, slot : slot + 1]
            low = pattern_ref[row : row + 1, slot : slot + 1]
            high = pattern_ref[row : row + 1, half_slots + slot : half_slots + slot + 1]
            code = row * total + low + (high - low) * h
            item_at = jnp.where(named & (rank_number == count), code, item_at)
            count = count + named.astype(jnp.int32)
    meta_v[me, 8:, :] = item_at
    for step in range(1, devices):
        meta_copy(step).start()

    def from_z(distance, way):
        source = z + way * distance
        valid = (source >= 0) & (source < n_row)
        position = source * n_col + x

        @pl.when(valid)
        def _():
            copy(position, 0, sibling, recv_sem).wait_recv()
        start(valid & (z - way >= 0) & (z - way < n_row), position, 0, device(z - way, x, h), recv_sem)
        start(valid, position, 1, device(z, across, h), recv_sem)
        start(valid, position, 2, sibling, sib_sem)

    def from_x(distance, way):
        source = z + way * distance
        valid = (source >= 0) & (source < n_row)
        position = source * n_col + across

        @pl.when(valid)
        def _():
            copy(position, 0, sibling, recv_sem).wait_recv()
        start(valid, position, 0, sibling, sib_sem)

    for distance in range(1, n_row):
        from_z(distance, 1)
        from_z(distance, -1)
        if distance == 1:
            from_x(0, 1)
        else:
            from_x(distance - 1, 1)
            from_x(distance - 1, -1)
    from_x(n_row - 1, 1)
    from_x(n_row - 1, -1)

    for step in range(1, devices):
        meta_copy(step).wait()
    local = pltpu.make_async_copy(meta_v, meta_s, local_sem)
    local.start()
    local.wait()
    for step in range(1, devices):
        position = lax.rem(me + step, devices)
        copy(position, 0, sibling, sib_sem, 1 - h).wait_recv()
    for valid, position, k, target, landed in sends:
        @pl.when(valid)
        def _(position=position, k=k, target=target, landed=landed):
            copy(position, k, target, landed).wait_send()

    lane = lax.broadcasted_iota(jnp.int32, (1, 2 * size), 1)

    def expand(source, carry):
        for row in range(rows):
            lanes = row // 2 * 2 * size
            at = row % 2 * size
            for pair in range(total // 2):
                slot = [meta_s[source, row, 2 * pair + t] for t in range(2)]
                both = [
                    packed[source, slot[t], :, lanes : lanes + 2 * size]
                    for t in range(2)
                ]
                spot = slice(pair * 2 * size, (pair + 1) * 2 * size)
                x_ref[pl.ds(pl.multiple_of(source * part + row * size, size), size), spot] = (
                    jnp.concatenate([both[t][:, at : at + size] for t in range(2)], axis=1)
                )
                kept = [(slot[t] < slots).astype(jnp.float32) for t in range(2)]
                mask_ref[source, row : row + 1, spot] = jnp.where(lane < size, kept[0], kept[1])
        return carry

    lax.fori_loop(0, devices, expand, 0)

    inv_scale = 1.0 / math.sqrt(size * slots)
    share = devices // 2

    def half_copy(side, step):
        ref = sq_ref.at[pl.ds((side * share + step) * part, part), :]
        return pltpu.make_async_remote_copy(
            src_ref=ref, dst_ref=ref, send_sem=sq_send.at[step], recv_sem=sq_recv.at[step],
            device_id=sibling, device_id_type=MESH,
        )

    def square(step, carry):
        source = h * share + step
        for d in range(-HOPS, HOPS + 1):
            own, spot, value = chunk_product(devices, part, x_ref, x_ref, source, d)
            kept = jnp.broadcast_to(mask_ref[source, :, spot][:, None, :], (rows, size, part))
            sq_ref[own, spot] = (value * inv_scale * kept.reshape(part, part)).astype(jnp.bfloat16)
        far = pl.ds(pl.multiple_of(lax.rem(source + HOPS + 1, devices) * part, part), part)
        sq_ref[own, far] = jnp.zeros((part, part), jnp.bfloat16)
        half_copy(h, step).start()
        return carry

    lax.fori_loop(0, share, square, 0)
    for step in range(share):
        half_copy(h, step).wait_send()
        half_copy(1 - h, step).wait_recv()


def chunk_product(devices, part, left_ref, right_ref, source, d):
    def chunk(r):
        return pl.ds(pl.multiple_of(lax.rem(source + r + devices, devices) * part, part), part)

    def apart(r):
        return min(r % devices, -r % devices)

    between = [r for r in range(-HOPS, HOPS + 1) if apart(r - d) <= HOPS]
    left = jnp.concatenate([left_ref[chunk(0), chunk(r)] for r in between], axis=1)
    right = jnp.concatenate([right_ref[chunk(r), chunk(d)] for r in between], axis=0)
    return chunk(0), chunk(d), jnp.dot(left, right, preferred_element_type=jnp.float32)


def dense_kernel(dims, x_ref, sq_ref, meta_s, out_ref, up_ref):
    n_row, n_col, rows, slots, size, capacity = dims
    devices = n_row * n_col
    total = devices * rows
    width = total * size
    part = rows * size
    me = lax.axis_index("row") * n_col + lax.axis_index("col")

    inv_scale = 1.0 / math.sqrt(size * slots)

    def cube(source, carry):
        for d in range(-HOPS, HOPS + 1):
            own, spot, value = chunk_product(devices, part, x_ref, sq_ref, source, d)
            value = 1.5 * x_ref[own, spot].astype(jnp.float32) - (0.5 * inv_scale) * value
            value = value.astype(jnp.bfloat16)
            column = lax.rem(source + d + devices, devices)
            for t in range(rows // 2):
                up_ref[column * (rows // 2) + t] = value[:, t * 2 * size : (t + 1) * 2 * size]
        for rank in range(capacity):
            code = meta_s[source, 8 + me, rank]
            found = jnp.maximum(code, 0)
            column = found & (total - 1)
            row = found >> (total.bit_length() - 1)
            block = up_ref[column >> 1, pl.ds(pl.multiple_of(row * size, size), size), :]
            block = block.astype(jnp.float32)
            block = jnp.where((column & 1) == 0, block[:, :size], block[:, size:])
            out_ref[source, rank] = jnp.where(code >= 0, block, 0.0).astype(jnp.bfloat16)
        return carry

    lax.fori_loop(0, devices, cube, 0)


def dense_shards(blocks, pattern, owner_map):
    rows, slots, size, _ = blocks.shape
    n_row, n_col = lax.axis_size("row"), lax.axis_size("col")
    devices = n_row * n_col
    total = devices * rows
    items = rows * (slots // 2)
    capacity = max(2, 3 * items // devices + 1)
    lanes = 128
    dims = (n_row, n_col, rows, slots, size, capacity)
    width = total * size
    vmem = pl.BlockSpec(memory_space=pltpu.VMEM)
    dense, squared, gathered_meta = pl.pallas_call(
        functools.partial(gather_kernel, dims),
        out_shape=(
            jax.ShapeDtypeStruct((width, width), jnp.bfloat16),
            jax.ShapeDtypeStruct((width, width), jnp.bfloat16),
            jax.ShapeDtypeStruct((devices, 16, lanes), jnp.int32),
        ),
        in_specs=[pl.BlockSpec(memory_space=pltpu.HBM), vmem, vmem],
        out_specs=(vmem, vmem, vmem),
        scratch_shapes=[
            pltpu.VMEM(blocks.shape, jnp.bfloat16),
            pltpu.VMEM((devices, slots + 1, size, rows * size), jnp.bfloat16),
            pltpu.SMEM((devices, 16, lanes), jnp.int32),
            pltpu.VMEM((devices, rows, width), jnp.float32),
            pltpu.SemaphoreType.DMA((devices, 3)),
            pltpu.SemaphoreType.DMA((devices,)),
            pltpu.SemaphoreType.DMA((devices,)),
            pltpu.SemaphoreType.DMA((devices,)),
            pltpu.SemaphoreType.DMA((devices,)),
            pltpu.SemaphoreType.DMA,
            pltpu.SemaphoreType.DMA((devices // 2,)),
            pltpu.SemaphoreType.DMA((devices // 2,)),
            pltpu.SemaphoreType.DMA,
        ],
        compiler_params=pltpu.CompilerParams(
            collective_id=0, has_side_effects=True, vmem_limit_bytes=32 * 1024 * 1024
        ),
    )(blocks, pattern, owner_map.reshape(rows, 1, slots // 2))
    out = pl.pallas_call(
        functools.partial(dense_kernel, dims),
        out_shape=jax.ShapeDtypeStruct((devices, capacity, size, size), jnp.bfloat16),
        in_specs=[vmem, vmem, pl.BlockSpec(memory_space=pltpu.SMEM)],
        out_specs=vmem,
        scratch_shapes=[pltpu.VMEM((total // 2, rows * size, 2 * size), jnp.bfloat16)],
        compiler_params=pltpu.CompilerParams(vmem_limit_bytes=28 * 1024 * 1024),
    )(dense, squared, gathered_meta)
    return out.reshape(1, 1, devices, capacity, size, size)


def solution(mesh):
    placed = (
        P(("groups", "row", "col"), None, None, None),
        P(("groups", "row", "col"), None),
        P("depth", ("groups", "row", "col"), None, None),
    )
    small = mesh.shape["row"] * mesh.shape["col"] == 8 and mesh.shape["col"] == 2
    return jax.shard_map(
        dense_shards if small else shards,
        mesh=mesh,
        in_specs=placed,
        out_specs=P("depth", ("groups", "row", "col"), None, None, None, None),
        check_vma=False,
    )
```

```python
import functools
import math

import jax
import jax.numpy as jnp
from jax import lax
from jax.experimental import pallas as pl
from jax.experimental.pallas import tpu as pltpu
from jax.sharding import PartitionSpec as P

HOPS = 3
MESH = pl.DeviceIdType.MESH


def passed_along(value, axis, by):
    peers = lax.axis_size(axis)
    return lax.ppermute(value, axis, [(i, (i + by) % peers) for i in range(peers)])


def product_rows(left, left_pattern, local_index, near_blocks, near_pattern, first_slot, slot_span):
    slot_count = left.shape[1]
    block_size = left.shape[2]

    def one_row(row_data):
        own_blocks, own_pattern, own_local = row_data
        used_local = lax.dynamic_slice_in_dim(own_local, first_slot, slot_span, 0)
        used_blocks = lax.dynamic_slice_in_dim(own_blocks, first_slot, slot_span, 0)
        fetched = jnp.take(near_blocks, used_local, axis=0).reshape(
            slot_span, slot_count, block_size * block_size
        )
        fetched_pattern = jnp.take(near_pattern, used_local, axis=0)
        select = (fetched_pattern[:, None, :] == own_pattern[None, :, None]).astype(jnp.bfloat16)
        aligned = jnp.einsum("kjl,klx->kjx", select, fetched, preferred_element_type=jnp.bfloat16)
        aligned = aligned.reshape(slot_span, slot_count, block_size, block_size)
        return jnp.einsum("kab,kjbc->jac", used_blocks, aligned, preferred_element_type=jnp.float32)

    return lax.map(one_row, (left, left_pattern, local_index))


def regroup(updated, targets):
    device_count = lax.axis_size(("row", "col"))
    row_count = updated.shape[0]
    half_slots = updated.shape[1]
    block_size = updated.shape[2]
    item_count = row_count * half_slots
    capacity = max(2, 3 * item_count // device_count + 1)
    flat_targets = targets.reshape(item_count)
    same_owner = flat_targets[:, None] == flat_targets[None, :]
    earlier = jnp.arange(item_count)[:, None] > jnp.arange(item_count)[None, :]
    rank_index = jnp.sum((same_owner & earlier).astype(jnp.int32), axis=1)
    destination = flat_targets * capacity + rank_index
    select = (
        jnp.arange(device_count * capacity, dtype=jnp.int32)[:, None] == destination[None, :]
    ).astype(jnp.bfloat16)
    outgoing = jnp.dot(
        select,
        updated.reshape(item_count, block_size * block_size),
        preferred_element_type=jnp.float32,
    ).astype(jnp.bfloat16)
    outgoing = outgoing.reshape(device_count, capacity, block_size, block_size)
    received = lax.all_to_all(outgoing, ("row", "col"), split_axis=0, concat_axis=0, tiled=True)
    return received.reshape(1, 1, device_count, capacity, block_size, block_size)


def shards(blocks, pattern, owner_map):
    row_count = blocks.shape[0]
    slot_count = blocks.shape[1]
    block_size = blocks.shape[2]
    half_slots = slot_count // 2
    device_count = lax.axis_size(("row", "col"))
    total_rows = device_count * row_count
    position = lax.axis_index(("row", "col"))
    layer_index = lax.axis_index("depth")
    inv_scale = 1.0 / math.sqrt(block_size * slot_count)
    targets = owner_map[0, :, :, 0]
    offsets = list(range(HOPS, 0, -1)) + list(range(-1, -HOPS - 1, -1))
    arrivals = [passed_along((blocks, pattern), ("row", "col"), offset) for offset in offsets]
    near_blocks = jnp.concatenate(
        [arrived[0] for arrived in arrivals[:HOPS]]
        + [blocks]
        + [arrived[0] for arrived in arrivals[HOPS:]],
        axis=0,
    )
    near_pattern = jnp.concatenate(
        [arrived[1] for arrived in arrivals[:HOPS]]
        + [pattern]
        + [arrived[1] for arrived in arrivals[HOPS:]],
        axis=0,
    )
    first_row = (position - HOPS) * row_count
    local_index = (pattern - first_row) % total_rows
    first_slot = layer_index * half_slots
    partial_value = product_rows(
        blocks, pattern, local_index, near_blocks, near_pattern, first_slot, half_slots
    )
    squared = (lax.psum(partial_value, "depth") * inv_scale).astype(jnp.bfloat16)
    w_arrivals = [passed_along(squared, ("row", "col"), offset) for offset in offsets]
    near_squared = jnp.concatenate(w_arrivals[:HOPS] + [squared] + w_arrivals[HOPS:], axis=0)
    partial_value = product_rows(
        blocks, pattern, local_index, near_squared, near_pattern, first_slot, half_slots
    )
    cubic_term = lax.psum_scatter(
        partial_value.astype(jnp.bfloat16), "depth", scatter_dimension=1, tiled=True
    ).astype(jnp.float32)
    own_blocks = lax.dynamic_slice_in_dim(blocks, first_slot, half_slots, 1)
    updated = (1.5 * own_blocks.astype(jnp.float32) - 0.5 * inv_scale * cubic_term).astype(
        jnp.bfloat16
    )
    return regroup(updated, targets)


def gather_kernel(
    dims, blocks_hbm, pattern_ref, owner_ref, x_ref, sq_ref, meta_v,
    blocks_ref, packed, meta_s, mask_ref,
    send_sem, recv_sem, sib_sem, meta_send, meta_recv, local_sem, sq_send, sq_recv, load_sem,
):
    n_row, n_col, rows, slots, size, capacity = dims
    devices = n_row * n_col
    total = devices * rows
    part = rows * size
    lanes = meta_v.shape[2]
    half_slots = slots // 2
    z, x, h = lax.axis_index("row"), lax.axis_index("col"), lax.axis_index("depth")
    me = z * n_col + x
    across = n_col - 1 - x

    def device(to_z, to_x, to_h):
        return {"row": to_z, "col": to_x, "depth": to_h}

    sibling = device(z, x, 1 - h)
    load = pltpu.make_async_copy(blocks_hbm, blocks_ref, load_sem)
    load.start()

    barrier = pltpu.get_barrier_semaphore()
    for step in range(1, devices):
        peer = lax.rem(me + step, devices)
        pl.semaphore_signal(
            barrier, inc=1, device_id=device(peer // n_col, lax.rem(peer, n_col), h),
            device_id_type=MESH,
        )
    pl.semaphore_signal(barrier, inc=1, device_id=sibling, device_id_type=MESH)

    for source in range(devices):
        packed[source, slots] = jnp.zeros((size, part), jnp.bfloat16)
    load.wait()
    for pair in range(rows // 2):
        packed[me, :slots, :, pair * 2 * size : (pair + 1) * 2 * size] = jnp.concatenate(
            [blocks_ref[2 * pair + t] for t in range(2)], axis=2
        )
    pl.semaphore_wait(barrier, devices)

    def meta_copy(step):
        peer = lax.rem(me + step, devices)
        return pltpu.make_async_remote_copy(
            src_ref=meta_v.at[me], dst_ref=meta_v.at[me],
            send_sem=meta_send.at[step], recv_sem=meta_recv.at[step],
            device_id=device(peer // n_col, lax.rem(peer, n_col), h), device_id_type=MESH,
        )

    bit = half_slots // 2

    def piece(position, which, q):
        return packed.at[position, pl.ds(which * half_slots + q * bit, bit)]

    def copy(position, k, q, target, landed, which=None):
        ref = piece(position, h if which is None else which, q)
        return pltpu.make_async_remote_copy(
            src_ref=ref, dst_ref=ref, send_sem=send_sem.at[position, k, q],
            recv_sem=landed.at[position, q], device_id=target, device_id_type=MESH,
        )

    sends = []

    def start(valid, *what):
        @pl.when(valid)
        def _():
            copy(*what).start()
        sends.append((valid, what))

    for q in range(2):
        start(z > 0, me, 0, q, device(z - 1, x, h), recv_sem)
        start(z < n_row - 1, me, 1, q, device(z + 1, x, h), recv_sem)
        start(z >= 0, me, 2, q, device(z, across, h), recv_sem)

    lane_number = lax.broadcasted_iota(jnp.int32, (rows, lanes), 1)
    slot_of = jnp.full((rows, lanes), slots, jnp.int32)
    for slot in range(slots):
        slot_of = jnp.where(pattern_ref[:, slot : slot + 1] == lane_number, slot, slot_of)
    meta_v[me, :rows, :] = slot_of
    meta_v[me, rows:8, :] = jnp.full((8 - rows, lanes), slots, jnp.int32)
    rank_number = lax.broadcasted_iota(jnp.int32, (devices, lanes), 1)
    owner_number = lax.broadcasted_iota(jnp.int32, (devices, lanes), 0)
    item_at = jnp.full((devices, lanes), -1, jnp.int32)
    count = jnp.zeros((devices, lanes), jnp.int32)
    for row in range(rows):
        for slot in range(half_slots):
            named = owner_number == owner_ref[row, :, slot : slot + 1]
            low = pattern_ref[row : row + 1, slot : slot + 1]
            high = pattern_ref[row : row + 1, half_slots + slot : half_slots + slot + 1]
            code = row * total + low + (high - low) * h
            item_at = jnp.where(named & (rank_number == count), code, item_at)
            count = count + named.astype(jnp.int32)
    meta_v[me, 8:, :] = item_at
    for step in range(1, devices):
        meta_copy(step).start()

    def from_z(distance, way, q):
        source = z + way * distance
        valid = (source >= 0) & (source < n_row)
        position = source * n_col + x

        @pl.when(valid)
        def _():
            copy(position, 0, q, sibling, recv_sem).wait_recv()
        start(valid & (z - way >= 0) & (z - way < n_row), position, 0, q, device(z - way, x, h), recv_sem)
        start(valid, position, 1, q, device(z, across, h), recv_sem)
        start(valid, position, 2, q, sibling, sib_sem)

    def from_x(distance, way, q):
        source = z + way * distance
        valid = (source >= 0) & (source < n_row)
        position = source * n_col + across

        @pl.when(valid)
        def _():
            copy(position, 0, q, sibling, recv_sem).wait_recv()
        start(valid, position, 0, q, sibling, sib_sem)

    for distance in range(1, n_row):
        for q in range(2):
            from_z(distance, 1, q)
            from_z(distance, -1, q)
            from_x(distance - 1, 1, q)
            if distance > 1:
                from_x(distance - 1, -1, q)
    for q in range(2):
        from_x(n_row - 1, 1, q)
        from_x(n_row - 1, -1, q)

    for step in range(1, devices):
        meta_copy(step).wait()
    local = pltpu.make_async_copy(meta_v, meta_s, local_sem)
    local.start()
    local.wait()
    for step in range(1, devices):
        position = lax.rem(me + step, devices)
        for q in range(2):
            copy(position, 0, q, sibling, sib_sem, 1 - h).wait_recv()
    for valid, what in sends:
        @pl.when(valid)
        def _(what=what):
            copy(*what).wait_send()

    lane = lax.broadcasted_iota(jnp.int32, (1, 2 * size), 1)

    def expand(source, carry):
        for row in range(rows):
            lanes = row // 2 * 2 * size
            at = row % 2 * size
            for pair in range(total // 2):
                slot = [meta_s[source, row, 2 * pair + t] for t in range(2)]
                both = [
                    packed[source, slot[t], :, lanes : lanes + 2 * size]
                    for t in range(2)
                ]
                spot = slice(pair * 2 * size, (pair + 1) * 2 * size)
                x_ref[pl.ds(pl.multiple_of(source * part + row * size, size), size), spot] = (
                    jnp.concatenate([both[t][:, at : at + size] for t in range(2)], axis=1)
                )
                kept = [(slot[t] < slots).astype(jnp.float32) for t in range(2)]
                mask_ref[source, row : row + 1, spot] = jnp.where(lane < size, kept[0], kept[1])
        return carry

    lax.fori_loop(0, devices, expand, 0)

    inv_scale = 1.0 / math.sqrt(size * slots)
    share = devices // 2

    def half_copy(side, step):
        ref = sq_ref.at[pl.ds((side * share + step) * part, part), :]
        return pltpu.make_async_remote_copy(
            src_ref=ref, dst_ref=ref, send_sem=sq_send.at[step], recv_sem=sq_recv.at[step],
            device_id=sibling, device_id_type=MESH,
        )

    def square(step, carry):
        source = h * share + step
        for d in range(-HOPS, HOPS + 1):
            own, spot, value = chunk_product(devices, part, x_ref, x_ref, source, d)
            kept = jnp.broadcast_to(mask_ref[source, :, spot][:, None, :], (rows, size, part))
            sq_ref[own, spot] = (value * inv_scale * kept.reshape(part, part)).astype(jnp.bfloat16)
        far = pl.ds(pl.multiple_of(lax.rem(source + HOPS + 1, devices) * part, part), part)
        sq_ref[own, far] = jnp.zeros((part, part), jnp.bfloat16)
        half_copy(h, step).start()
        return carry

    lax.fori_loop(0, share, square, 0)
    for step in range(share):
        half_copy(h, step).wait_send()
        half_copy(1 - h, step).wait_recv()


def chunk_product(devices, part, left_ref, right_ref, source, d):
    def chunk(r):
        return pl.ds(pl.multiple_of(lax.rem(source + r + devices, devices) * part, part), part)

    def apart(r):
        return min(r % devices, -r % devices)

    between = [r for r in range(-HOPS, HOPS + 1) if apart(r - d) <= HOPS]
    left = jnp.concatenate([left_ref[chunk(0), chunk(r)] for r in between], axis=1)
    right = jnp.concatenate([right_ref[chunk(r), chunk(d)] for r in between], axis=0)
    return chunk(0), chunk(d), jnp.dot(left, right, preferred_element_type=jnp.float32)


def dense_kernel(dims, x_ref, sq_ref, meta_s, out_ref, up_ref):
    n_row, n_col, rows, slots, size, capacity = dims
    devices = n_row * n_col
    total = devices * rows
    width = total * size
    part = rows * size
    me = lax.axis_index("row") * n_col + lax.axis_index("col")

    inv_scale = 1.0 / math.sqrt(size * slots)

    def cube(source, carry):
        for d in range(-HOPS, HOPS + 1):
            own, spot, value = chunk_product(devices, part, x_ref, sq_ref, source, d)
            value = 1.5 * x_ref[own, spot].astype(jnp.float32) - (0.5 * inv_scale) * value
            value = value.astype(jnp.bfloat16)
            column = lax.rem(source + d + devices, devices)
            for t in range(rows // 2):
                up_ref[column * (rows // 2) + t] = value[:, t * 2 * size : (t + 1) * 2 * size]
        for rank in range(capacity):
            code = meta_s[source, 8 + me, rank]
            found = jnp.maximum(code, 0)
            column = found & (total - 1)
            row = found >> (total.bit_length() - 1)
            block = up_ref[column >> 1, pl.ds(pl.multiple_of(row * size, size), size), :]
            block = block.astype(jnp.float32)
            block = jnp.where((column & 1) == 0, block[:, :size], block[:, size:])
            out_ref[source, rank] = jnp.where(code >= 0, block, 0.0).astype(jnp.bfloat16)
        return carry

    lax.fori_loop(0, devices, cube, 0)


def dense_shards(blocks, pattern, owner_map):
    rows, slots, size, _ = blocks.shape
    n_row, n_col = lax.axis_size("row"), lax.axis_size("col")
    devices = n_row * n_col
    total = devices * rows
    items = rows * (slots // 2)
    capacity = max(2, 3 * items // devices + 1)
    lanes = 128
    dims = (n_row, n_col, rows, slots, size, capacity)
    width = total * size
    vmem = pl.BlockSpec(memory_space=pltpu.VMEM)
    dense, squared, gathered_meta = pl.pallas_call(
        functools.partial(gather_kernel, dims),
        out_shape=(
            jax.ShapeDtypeStruct((width, width), jnp.bfloat16),
            jax.ShapeDtypeStruct((width, width), jnp.bfloat16),
            jax.ShapeDtypeStruct((devices, 16, lanes), jnp.int32),
        ),
        in_specs=[pl.BlockSpec(memory_space=pltpu.HBM), vmem, vmem],
        out_specs=(vmem, vmem, vmem),
        scratch_shapes=[
            pltpu.VMEM(blocks.shape, jnp.bfloat16),
            pltpu.VMEM((devices, slots + 1, size, rows * size), jnp.bfloat16),
            pltpu.SMEM((devices, 16, lanes), jnp.int32),
            pltpu.VMEM((devices, rows, width), jnp.float32),
            pltpu.SemaphoreType.DMA((devices, 3, 2)),
            pltpu.SemaphoreType.DMA((devices, 2)),
            pltpu.SemaphoreType.DMA((devices, 2)),
            pltpu.SemaphoreType.DMA((devices,)),
            pltpu.SemaphoreType.DMA((devices,)),
            pltpu.SemaphoreType.DMA,
            pltpu.SemaphoreType.DMA((devices // 2,)),
            pltpu.SemaphoreType.DMA((devices // 2,)),
            pltpu.SemaphoreType.DMA,
        ],
        compiler_params=pltpu.CompilerParams(
            collective_id=0, has_side_effects=True, vmem_limit_bytes=32 * 1024 * 1024
        ),
    )(blocks, pattern, owner_map.reshape(rows, 1, slots // 2))
    out = pl.pallas_call(
        functools.partial(dense_kernel, dims),
        out_shape=jax.ShapeDtypeStruct((devices, capacity, size, size), jnp.bfloat16),
        in_specs=[vmem, vmem, pl.BlockSpec(memory_space=pltpu.SMEM)],
        out_specs=vmem,
        scratch_shapes=[pltpu.VMEM((total // 2, rows * size, 2 * size), jnp.bfloat16)],
        compiler_params=pltpu.CompilerParams(vmem_limit_bytes=28 * 1024 * 1024),
    )(dense, squared, gathered_meta)
    return out.reshape(1, 1, devices, capacity, size, size)


def solution(mesh):
    placed = (
        P(("groups", "row", "col"), None, None, None),
        P(("groups", "row", "col"), None),
        P("depth", ("groups", "row", "col"), None, None),
    )
    small = mesh.shape["row"] * mesh.shape["col"] == 8 and mesh.shape["col"] == 2
    return jax.shard_map(
        dense_shards if small else shards,
        mesh=mesh,
        in_specs=placed,
        out_specs=P("depth", ("groups", "row", "col"), None, None, None, None),
        check_vma=False,
    )
```

```python
import functools
import math

import jax
import jax.numpy as jnp
from jax import lax
from jax.experimental import pallas as pl
from jax.experimental.pallas import tpu as pltpu
from jax.sharding import PartitionSpec as P

HOPS = 3
MESH = pl.DeviceIdType.MESH


def passed_along(value, axis, by):
    peers = lax.axis_size(axis)
    return lax.ppermute(value, axis, [(i, (i + by) % peers) for i in range(peers)])


def product_rows(left, left_pattern, local_index, near_blocks, near_pattern, first_slot, slot_span):
    slot_count = left.shape[1]
    block_size = left.shape[2]

    def one_row(row_data):
        own_blocks, own_pattern, own_local = row_data
        used_local = lax.dynamic_slice_in_dim(own_local, first_slot, slot_span, 0)
        used_blocks = lax.dynamic_slice_in_dim(own_blocks, first_slot, slot_span, 0)
        fetched = jnp.take(near_blocks, used_local, axis=0).reshape(
            slot_span, slot_count, block_size * block_size
        )
        fetched_pattern = jnp.take(near_pattern, used_local, axis=0)
        select = (fetched_pattern[:, None, :] == own_pattern[None, :, None]).astype(jnp.bfloat16)
        aligned = jnp.einsum("kjl,klx->kjx", select, fetched, preferred_element_type=jnp.bfloat16)
        aligned = aligned.reshape(slot_span, slot_count, block_size, block_size)
        return jnp.einsum("kab,kjbc->jac", used_blocks, aligned, preferred_element_type=jnp.float32)

    return lax.map(one_row, (left, left_pattern, local_index))


def regroup(updated, targets):
    device_count = lax.axis_size(("row", "col"))
    row_count = updated.shape[0]
    half_slots = updated.shape[1]
    block_size = updated.shape[2]
    item_count = row_count * half_slots
    capacity = max(2, 3 * item_count // device_count + 1)
    flat_targets = targets.reshape(item_count)
    same_owner = flat_targets[:, None] == flat_targets[None, :]
    earlier = jnp.arange(item_count)[:, None] > jnp.arange(item_count)[None, :]
    rank_index = jnp.sum((same_owner & earlier).astype(jnp.int32), axis=1)
    destination = flat_targets * capacity + rank_index
    select = (
        jnp.arange(device_count * capacity, dtype=jnp.int32)[:, None] == destination[None, :]
    ).astype(jnp.bfloat16)
    outgoing = jnp.dot(
        select,
        updated.reshape(item_count, block_size * block_size),
        preferred_element_type=jnp.float32,
    ).astype(jnp.bfloat16)
    outgoing = outgoing.reshape(device_count, capacity, block_size, block_size)
    received = lax.all_to_all(outgoing, ("row", "col"), split_axis=0, concat_axis=0, tiled=True)
    return received.reshape(1, 1, device_count, capacity, block_size, block_size)


def shards(blocks, pattern, owner_map):
    row_count = blocks.shape[0]
    slot_count = blocks.shape[1]
    block_size = blocks.shape[2]
    half_slots = slot_count // 2
    device_count = lax.axis_size(("row", "col"))
    total_rows = device_count * row_count
    position = lax.axis_index(("row", "col"))
    layer_index = lax.axis_index("depth")
    inv_scale = 1.0 / math.sqrt(block_size * slot_count)
    targets = owner_map[0, :, :, 0]
    offsets = list(range(HOPS, 0, -1)) + list(range(-1, -HOPS - 1, -1))
    arrivals = [passed_along((blocks, pattern), ("row", "col"), offset) for offset in offsets]
    near_blocks = jnp.concatenate(
        [arrived[0] for arrived in arrivals[:HOPS]]
        + [blocks]
        + [arrived[0] for arrived in arrivals[HOPS:]],
        axis=0,
    )
    near_pattern = jnp.concatenate(
        [arrived[1] for arrived in arrivals[:HOPS]]
        + [pattern]
        + [arrived[1] for arrived in arrivals[HOPS:]],
        axis=0,
    )
    first_row = (position - HOPS) * row_count
    local_index = (pattern - first_row) % total_rows
    first_slot = layer_index * half_slots
    partial_value = product_rows(
        blocks, pattern, local_index, near_blocks, near_pattern, first_slot, half_slots
    )
    squared = (lax.psum(partial_value, "depth") * inv_scale).astype(jnp.bfloat16)
    w_arrivals = [passed_along(squared, ("row", "col"), offset) for offset in offsets]
    near_squared = jnp.concatenate(w_arrivals[:HOPS] + [squared] + w_arrivals[HOPS:], axis=0)
    partial_value = product_rows(
        blocks, pattern, local_index, near_squared, near_pattern, first_slot, half_slots
    )
    cubic_term = lax.psum_scatter(
        partial_value.astype(jnp.bfloat16), "depth", scatter_dimension=1, tiled=True
    ).astype(jnp.float32)
    own_blocks = lax.dynamic_slice_in_dim(blocks, first_slot, half_slots, 1)
    updated = (1.5 * own_blocks.astype(jnp.float32) - 0.5 * inv_scale * cubic_term).astype(
        jnp.bfloat16
    )
    return regroup(updated, targets)


def gather_kernel(
    dims, blocks_hbm, pattern_ref, owner_ref, x_ref, sq_ref, meta_v,
    blocks_ref, packed, meta_s, mask_ref,
    send_sem, recv_sem, sib_sem, meta_send, meta_recv, local_sem, sq_send, sq_recv, load_sem,
):
    n_row, n_col, rows, slots, size, capacity = dims
    devices = n_row * n_col
    total = devices * rows
    part = rows * size
    lanes = meta_v.shape[2]
    half_slots = slots // 2
    z, x, h = lax.axis_index("row"), lax.axis_index("col"), lax.axis_index("depth")
    me = z * n_col + x
    across = n_col - 1 - x

    def device(to_z, to_x, to_h):
        return {"row": to_z, "col": to_x, "depth": to_h}

    sibling = device(z, x, 1 - h)
    load = pltpu.make_async_copy(blocks_hbm, blocks_ref, load_sem)
    load.start()

    barrier = pltpu.get_barrier_semaphore()
    for step in range(1, devices):
        peer = lax.rem(me + step, devices)
        pl.semaphore_signal(
            barrier, inc=1, device_id=device(peer // n_col, lax.rem(peer, n_col), h),
            device_id_type=MESH,
        )
    pl.semaphore_signal(barrier, inc=1, device_id=sibling, device_id_type=MESH)

    for source in range(devices):
        packed[source, slots] = jnp.zeros((size, part), jnp.bfloat16)
    load.wait()
    for pair in range(rows // 2):
        packed[me, :slots, :, pair * 2 * size : (pair + 1) * 2 * size] = jnp.concatenate(
            [blocks_ref[2 * pair + t] for t in range(2)], axis=2
        )
    pl.semaphore_wait(barrier, devices)

    def meta_copy(step):
        peer = lax.rem(me + step, devices)
        return pltpu.make_async_remote_copy(
            src_ref=meta_v.at[me], dst_ref=meta_v.at[me],
            send_sem=meta_send.at[step], recv_sem=meta_recv.at[step],
            device_id=device(peer // n_col, lax.rem(peer, n_col), h), device_id_type=MESH,
        )

    bit = half_slots // 2

    def piece(position, which, q):
        return packed.at[position, pl.ds(which * half_slots + q * bit, bit)]

    def copy(position, k, q, target, landed, which=None):
        ref = piece(position, h if which is None else which, q)
        return pltpu.make_async_remote_copy(
            src_ref=ref, dst_ref=ref, send_sem=send_sem.at[position, k, q],
            recv_sem=landed.at[position, q], device_id=target, device_id_type=MESH,
        )

    sends = []

    def start(valid, *what):
        @pl.when(valid)
        def _():
            copy(*what).start()
        sends.append((valid, what))

    for q in range(2):
        start(z > 0, me, 0, q, device(z - 1, x, h), recv_sem)
        start(z < n_row - 1, me, 1, q, device(z + 1, x, h), recv_sem)
        start(z >= 0, me, 2, q, device(z, across, h), recv_sem)

    lane_number = lax.broadcasted_iota(jnp.int32, (rows, lanes), 1)
    slot_of = jnp.full((rows, lanes), slots, jnp.int32)
    for slot in range(slots):
        slot_of = jnp.where(pattern_ref[:, slot : slot + 1] == lane_number, slot, slot_of)
    meta_v[me, :rows, :] = slot_of
    meta_v[me, rows:8, :] = jnp.full((8 - rows, lanes), slots, jnp.int32)
    rank_number = lax.broadcasted_iota(jnp.int32, (devices, lanes), 1)
    owner_number = lax.broadcasted_iota(jnp.int32, (devices, lanes), 0)
    item_at = jnp.full((devices, lanes), -1, jnp.int32)
    count = jnp.zeros((devices, lanes), jnp.int32)
    for row in range(rows):
        for slot in range(half_slots):
            named = owner_number == owner_ref[row, :, slot : slot + 1]
            low = pattern_ref[row : row + 1, slot : slot + 1]
            high = pattern_ref[row : row + 1, half_slots + slot : half_slots + slot + 1]
            code = row * total + low + (high - low) * h
            item_at = jnp.where(named & (rank_number == count), code, item_at)
            count = count + named.astype(jnp.int32)
    meta_v[me, 8:, :] = item_at
    for step in range(1, devices):
        meta_copy(step).start()

    def from_z(distance, way, q):
        source = z + way * distance
        valid = (source >= 0) & (source < n_row)
        position = source * n_col + x

        @pl.when(valid)
        def _():
            copy(position, 0, q, sibling, recv_sem).wait_recv()
        start(valid & (z - way >= 0) & (z - way < n_row), position, 0, q, device(z - way, x, h), recv_sem)
        crossing = valid
        if q == 1 and distance == 1:
            crossing = valid & (source > 0) & (source < n_row - 1)
        if q == 0 or distance < n_row - 1:
            start(crossing, position, 1, q, device(z, across, h), recv_sem)
        start(valid, position, 2, q, sibling, sib_sem)

    def from_x(distance, way, q):
        source = z + way * distance
        valid = (source >= 0) & (source < n_row)
        position = source * n_col + across

        @pl.when(valid)
        def _():
            copy(position, 0, q, sibling, recv_sem).wait_recv()
        if q == 1 and distance in (0, n_row - 2):
            up = valid & (source == 0) & (z == distance)
            down = valid & (source == n_row - 1) & (z == n_row - 1 - distance)
            start(up, position, 1, q, device(z + 1, x, h), recv_sem)
            start(down, position, 1, q, device(z - 1, x, h), recv_sem)
        start(valid, position, 0, q, sibling, sib_sem)

    for distance in range(1, n_row):
        for q in range(2):
            from_z(distance, 1, q)
            from_z(distance, -1, q)
            from_x(distance - 1, 1, q)
            if distance > 1:
                from_x(distance - 1, -1, q)
    for q in range(2):
        from_x(n_row - 1, 1, q)
        from_x(n_row - 1, -1, q)

    for step in range(1, devices):
        meta_copy(step).wait()
    local = pltpu.make_async_copy(meta_v, meta_s, local_sem)
    local.start()
    local.wait()
    for step in range(1, devices):
        position = lax.rem(me + step, devices)
        for q in range(2):
            copy(position, 0, q, sibling, sib_sem, 1 - h).wait_recv()
    for valid, what in sends:
        @pl.when(valid)
        def _(what=what):
            copy(*what).wait_send()

    lane = lax.broadcasted_iota(jnp.int32, (1, 2 * size), 1)

    def expand(source, carry):
        for row in range(rows):
            lanes = row // 2 * 2 * size
            at = row % 2 * size
            for pair in range(total // 2):
                slot = [meta_s[source, row, 2 * pair + t] for t in range(2)]
                both = [
                    packed[source, slot[t], :, lanes : lanes + 2 * size]
                    for t in range(2)
                ]
                spot = slice(pair * 2 * size, (pair + 1) * 2 * size)
                x_ref[pl.ds(pl.multiple_of(source * part + row * size, size), size), spot] = (
                    jnp.concatenate([both[t][:, at : at + size] for t in range(2)], axis=1)
                )
                kept = [(slot[t] < slots).astype(jnp.float32) for t in range(2)]
                mask_ref[source, row : row + 1, spot] = jnp.where(lane < size, kept[0], kept[1])
        return carry

    lax.fori_loop(0, devices, expand, 0)

    inv_scale = 1.0 / math.sqrt(size * slots)
    share = devices // 2

    def half_copy(side, step):
        ref = sq_ref.at[pl.ds((side * share + step) * part, part), :]
        return pltpu.make_async_remote_copy(
            src_ref=ref, dst_ref=ref, send_sem=sq_send.at[step], recv_sem=sq_recv.at[step],
            device_id=sibling, device_id_type=MESH,
        )

    def square(step, carry):
        source = h * share + step
        for d in range(-HOPS, HOPS + 1):
            own, spot, value = chunk_product(devices, part, x_ref, x_ref, source, d)
            kept = jnp.broadcast_to(mask_ref[source, :, spot][:, None, :], (rows, size, part))
            sq_ref[own, spot] = (value * inv_scale * kept.reshape(part, part)).astype(jnp.bfloat16)
        far = pl.ds(pl.multiple_of(lax.rem(source + HOPS + 1, devices) * part, part), part)
        sq_ref[own, far] = jnp.zeros((part, part), jnp.bfloat16)
        half_copy(h, step).start()
        return carry

    lax.fori_loop(0, share, square, 0)
    for step in range(share):
        half_copy(h, step).wait_send()
        half_copy(1 - h, step).wait_recv()


def chunk_product(devices, part, left_ref, right_ref, source, d):
    def chunk(r):
        return pl.ds(pl.multiple_of(lax.rem(source + r + devices, devices) * part, part), part)

    def apart(r):
        return min(r % devices, -r % devices)

    between = [r for r in range(-HOPS, HOPS + 1) if apart(r - d) <= HOPS]
    left = jnp.concatenate([left_ref[chunk(0), chunk(r)] for r in between], axis=1)
    right = jnp.concatenate([right_ref[chunk(r), chunk(d)] for r in between], axis=0)
    return chunk(0), chunk(d), jnp.dot(left, right, preferred_element_type=jnp.float32)


def dense_kernel(dims, x_ref, sq_ref, meta_s, out_ref, up_ref):
    n_row, n_col, rows, slots, size, capacity = dims
    devices = n_row * n_col
    total = devices * rows
    width = total * size
    part = rows * size
    me = lax.axis_index("row") * n_col + lax.axis_index("col")

    inv_scale = 1.0 / math.sqrt(size * slots)

    def cube(source, carry):
        for d in range(-HOPS, HOPS + 1):
            own, spot, value = chunk_product(devices, part, x_ref, sq_ref, source, d)
            value = 1.5 * x_ref[own, spot].astype(jnp.float32) - (0.5 * inv_scale) * value
            value = value.astype(jnp.bfloat16)
            column = lax.rem(source + d + devices, devices)
            for t in range(rows // 2):
                up_ref[column * (rows // 2) + t] = value[:, t * 2 * size : (t + 1) * 2 * size]
        for rank in range(capacity):
            code = meta_s[source, 8 + me, rank]
            found = jnp.maximum(code, 0)
            column = found & (total - 1)
            row = found >> (total.bit_length() - 1)
            block = up_ref[column >> 1, pl.ds(pl.multiple_of(row * size, size), size), :]
            block = block.astype(jnp.float32)
            block = jnp.where((column & 1) == 0, block[:, :size], block[:, size:])
            out_ref[source, rank] = jnp.where(code >= 0, block, 0.0).astype(jnp.bfloat16)
        return carry

    lax.fori_loop(0, devices, cube, 0)


def dense_shards(blocks, pattern, owner_map):
    rows, slots, size, _ = blocks.shape
    n_row, n_col = lax.axis_size("row"), lax.axis_size("col")
    devices = n_row * n_col
    total = devices * rows
    items = rows * (slots // 2)
    capacity = max(2, 3 * items // devices + 1)
    lanes = 128
    dims = (n_row, n_col, rows, slots, size, capacity)
    width = total * size
    vmem = pl.BlockSpec(memory_space=pltpu.VMEM)
    dense, squared, gathered_meta = pl.pallas_call(
        functools.partial(gather_kernel, dims),
        out_shape=(
            jax.ShapeDtypeStruct((width, width), jnp.bfloat16),
            jax.ShapeDtypeStruct((width, width), jnp.bfloat16),
            jax.ShapeDtypeStruct((devices, 16, lanes), jnp.int32),
        ),
        in_specs=[pl.BlockSpec(memory_space=pltpu.HBM), vmem, vmem],
        out_specs=(vmem, vmem, vmem),
        scratch_shapes=[
            pltpu.VMEM(blocks.shape, jnp.bfloat16),
            pltpu.VMEM((devices, slots + 1, size, rows * size), jnp.bfloat16),
            pltpu.SMEM((devices, 16, lanes), jnp.int32),
            pltpu.VMEM((devices, rows, width), jnp.float32),
            pltpu.SemaphoreType.DMA((devices, 3, 2)),
            pltpu.SemaphoreType.DMA((devices, 2)),
            pltpu.SemaphoreType.DMA((devices, 2)),
            pltpu.SemaphoreType.DMA((devices,)),
            pltpu.SemaphoreType.DMA((devices,)),
            pltpu.SemaphoreType.DMA,
            pltpu.SemaphoreType.DMA((devices // 2,)),
            pltpu.SemaphoreType.DMA((devices // 2,)),
            pltpu.SemaphoreType.DMA,
        ],
        compiler_params=pltpu.CompilerParams(
            collective_id=0, has_side_effects=True, vmem_limit_bytes=32 * 1024 * 1024
        ),
    )(blocks, pattern, owner_map.reshape(rows, 1, slots // 2))
    out = pl.pallas_call(
        functools.partial(dense_kernel, dims),
        out_shape=jax.ShapeDtypeStruct((devices, capacity, size, size), jnp.bfloat16),
        in_specs=[vmem, vmem, pl.BlockSpec(memory_space=pltpu.SMEM)],
        out_specs=vmem,
        scratch_shapes=[pltpu.VMEM((total // 2, rows * size, 2 * size), jnp.bfloat16)],
        compiler_params=pltpu.CompilerParams(vmem_limit_bytes=28 * 1024 * 1024),
    )(dense, squared, gathered_meta)
    return out.reshape(1, 1, devices, capacity, size, size)


def solution(mesh):
    placed = (
        P(("groups", "row", "col"), None, None, None),
        P(("groups", "row", "col"), None),
        P("depth", ("groups", "row", "col"), None, None),
    )
    small = mesh.shape["row"] * mesh.shape["col"] == 8 and mesh.shape["col"] == 2
    return jax.shard_map(
        dense_shards if small else shards,
        mesh=mesh,
        in_specs=placed,
        out_specs=P("depth", ("groups", "row", "col"), None, None, None, None),
        check_vma=False,
    )
```
